256 devices in a mesh: seq: 128 (over x, y, z), head: 2 (over core).
Axes of the slice: x: 4, y: 4, z: 8, core: 2. Of those that a mesh axis runs over, the one named last changes fastest.
Arguments:
- query: bfloat16 [32768, 1024], P('seq', 'head'), may hold values from -8 to 8
- key: bfloat16 [32768, 1024], P('seq', 'head'), may hold values from -8 to 8
- value: bfloat16 [32768, 1024], P('seq', 'head'), may hold values from -8 to 8
- grad_out: bfloat16 [32768, 1024], P('seq', 'head'), may hold values from -64 to 64
- out_weight: bfloat16 [1024, 1024], P('head'), may hold values from -0.1875 to 0.1875
Outputs:
- mixed: bfloat16 [32768, 1024], P('seq', 'head')
- grad_query: bfloat16 [32768, 1024], P('seq', 'head')
- grad_key: bfloat16 [32768, 1024], P('seq', 'head')
- grad_value: bfloat16 [32768, 1024], P('seq', 'head')
- grad_weight: float32 [1024, 1024], P('head')
The draws below stay inside these ranges and needn't reach their ends.
All inputs are finite; a program needn't handle non-finite values.
Results may differ from the reference program's by a relative error of at most 0.0079.
Values may be sent and summed in bfloat16 or wider, within the bound.
No kernel may reach another device: no remote copies, remote signals or barrier semaphores. Data moves between devices by JAX's collectives and lax.ppermute only.
A program may use at most 128 MiB of HBM per device.

```python
import jax
import jax.numpy as jnp
from jax import lax

HEADS = 16
HEAD_DIM = 64
WIDTH = 1024
POOL = 128
TOK_DEV = 256
TOKENS = 32768
N_SEQ = 128


def base_field(key, amplitude):
    columns = HEADS * HEAD_DIM
    streams = jax.random.split(key, 24)
    field = jax.random.normal(streams[0], (TOKENS, columns), jnp.float32)
    span = POOL
    stream_index = 1
    while span <= TOKENS // 2:
        table = jax.random.normal(streams[stream_index], (TOKENS // span, 1, columns), jnp.float32) * amplitude
        field = (field.reshape(TOKENS // span, span, columns) + table).reshape(TOKENS, columns)
        span = span * 2
        stream_index = stream_index + 1
    return field


def draw_query(key, part):
    amplitude = 0.3
    field = base_field(jax.random.fold_in(key, 11), amplitude)
    return jnp.clip(field, -8.0, 8.0).astype(jnp.bfloat16)


def draw_key(key, part):
    amplitude = 0.3
    field = base_field(jax.random.fold_in(key, 12), amplitude)
    return jnp.clip(field, -8.0, 8.0).astype(jnp.bfloat16)


def draw_value(key, part):
    amplitude = 0.3
    field = base_field(jax.random.fold_in(key, 13), amplitude)
    return jnp.clip(field, -8.0, 8.0).astype(jnp.bfloat16)


def draw_grad_out(key, part):
    amplitude = 0.3
    field = base_field(jax.random.fold_in(key, 14), amplitude) * 8.0
    return jnp.clip(field, -64.0, 64.0).astype(jnp.bfloat16)


def shard_levels(rng, extent, pieces, smallest, high):
    def one(axis_at, parts):
        heights = jax.random.uniform(jax.random.fold_in(jax.random.fold_in(rng, 6), axis_at), (parts,), jnp.float32, smallest / len(pieces), high / len(pieces))
        return jnp.repeat(jnp.exp(heights), extent[axis_at] // parts).reshape((-1,) + (1,) * (len(extent) - axis_at - 1))

    gain = one(*pieces[0])
    for cut in pieces[1:]:
        gain = gain * one(*cut)
    return gain


def normal_values(key, extent, spread, reach, cuts=(), kind=jnp.bfloat16):
    gain = shard_levels(key, extent, cuts, -0.22, 0.18) if cuts else 1.0
    entries = jax.random.normal(key, extent, jnp.float32) * spread * gain
    return jnp.minimum(jnp.maximum(entries, -reach), reach).astype(kind)


def setup_inputs(seed: int = 0) -> dict:
    streams_of = jax.random.split(jax.random.key(seed), 6)
    return {
        "query": draw_query(jax.random.fold_in(streams_of[5], 71), 0),
        "key": draw_key(jax.random.fold_in(streams_of[5], 71), 0),
        "value": draw_value(jax.random.fold_in(streams_of[5], 71), 0),
        "grad_out": draw_grad_out(jax.random.fold_in(streams_of[5], 71), 0),
        "out_weight": normal_values(streams_of[4], (WIDTH, WIDTH), WIDTH ** -0.5, 0.1875, ((0, 2),)),
    }


def product(form, left, right):
    return jnp.einsum(form, left.astype(jnp.float32), right.astype(jnp.float32))


def pool_pairs(values, along):
    shaped = values.shape
    paired = values.reshape(shaped[:along] + (shaped[along] // 2, 2) + shaped[along + 1:]).astype(jnp.float32)
    return (jnp.sum(paired, axis=along + 1) * 0.5).astype(jnp.bfloat16)


def spread_pairs(gradients, along):
    return jnp.repeat(gradients * 0.5, 2, axis=along)


def build_levels(values, local_depth):
    levels = [values]
    for height_index in range(local_depth):
        levels.append(pool_pairs(levels[-1], 0))
    return levels


def arrange_near(levels, blocks, columns):
    portions = [levels[0].reshape(blocks, POOL, columns)]
    for height_index in range(len(levels)):
        subtree = levels[height_index].reshape(blocks >> height_index, POOL, columns)
        swapped = subtree.reshape(blocks >> (height_index + 1), 2, POOL, columns)[:, ::-1]
        swapped = swapped.reshape(blocks >> height_index, POOL, columns)
        portions.append(jnp.repeat(swapped, 1 << height_index, axis=0))
    return jnp.concatenate(portions, axis=1)


def fold_back(gradients, local_depth, tokens_here, columns):
    blocks = tokens_here // POOL
    own_part = gradients[:, :POOL].reshape(tokens_here, columns)
    running = None
    for height_index in reversed(range(local_depth)):
        portion = gradients[:, (height_index + 1) * POOL:(height_index + 2) * POOL]
        portion = jnp.sum(portion.reshape(blocks >> height_index, 1 << height_index, POOL, columns), axis=1)
        portion = portion.reshape(blocks >> (height_index + 1), 2, POOL, columns)[:, ::-1]
        portion = portion.reshape(tokens_here >> height_index, columns)
        if running is not None:
            portion = portion + spread_pairs(running, 0)
        running = portion
    return running + own_part


def device_attention(query, key_levels, value_levels, grad_in, far_key, far_value):
    tokens_here, columns = query.shape
    blocks = tokens_here // POOL
    local_depth = len(key_levels)
    near_key = arrange_near(key_levels, blocks, columns)
    near_value = arrange_near(value_levels, blocks, columns)
    near_count = near_key.shape[1]
    far_count = far_key.shape[0]
    group_width = 2 * HEAD_DIM
    score_scale = HEAD_DIM ** -0.5
    query_blocks = query.reshape(blocks, POOL, columns)
    grad_blocks = grad_in.reshape(blocks, POOL, columns)

    def one_group(group_index, buffers):
        column_start = group_index * group_width

        def columns_of(source):
            return lax.dynamic_slice_in_dim(source, column_start, group_width, source.ndim - 1)

        def split_heads(source):
            return source.reshape(source.shape[:-1] + (2, HEAD_DIM))

        def joined(source):
            return source.reshape(source.shape[:-2] + (group_width,))

        query_heads = split_heads(columns_of(query_blocks))
        grad_heads = split_heads(columns_of(grad_blocks))
        near_keys = split_heads(columns_of(near_key))
        near_values = split_heads(columns_of(near_value))
        far_keys = split_heads(columns_of(far_key))
        far_values = split_heads(columns_of(far_value))
        scores = jnp.concatenate((product("bqhd,bkhd->bhqk", query_heads, near_keys), product("bqhd,khd->bhqk", query_heads, far_keys)), axis=3) * score_scale
        highest = jnp.max(scores, axis=3, keepdims=True)
        weights = jnp.exp(scores - highest)
        probabilities = weights / jnp.sum(weights, axis=3, keepdims=True)
        rounded = probabilities.astype(jnp.bfloat16)
        rounded_near = rounded[..., :near_count]
        rounded_far = rounded[..., near_count:]
        attended = (product("bhqk,bkhd->bqhd", rounded_near, near_values) + product("bhqk,khd->bqhd", rounded_far, far_values)).astype(jnp.bfloat16)
        grad_probs = jnp.concatenate((product("bqhd,bkhd->bhqk", grad_heads, near_values), product("bqhd,khd->bhqk", grad_heads, far_values)), axis=3)
        centred = jnp.sum(probabilities * grad_probs, axis=3, keepdims=True)
        grad_scores = (probabilities * (grad_probs - centred) * score_scale).astype(jnp.bfloat16)
        scores_near = grad_scores[..., :near_count]
        scores_far = grad_scores[..., near_count:]
        grad_query = (product("bhqk,bkhd->bqhd", scores_near, near_keys) + product("bhqk,khd->bqhd", scores_far, far_keys)).astype(jnp.bfloat16)
        fresh = (joined(attended), joined(grad_query),
                 joined(product("bhqk,bqhd->bkhd", scores_near, query_heads)),
                 joined(product("bhqk,bqhd->bkhd", rounded_near, grad_heads)),
                 joined(product("bhqk,bqhd->khd", scores_far, query_heads)),
                 joined(product("bhqk,bqhd->khd", rounded_far, grad_heads)))
        return tuple(lax.dynamic_update_slice_in_dim(buffer, update, column_start, buffer.ndim - 1) for buffer, update in zip(buffers, fresh))

    initial = (jnp.zeros((blocks, POOL, columns), jnp.bfloat16), jnp.zeros((blocks, POOL, columns), jnp.bfloat16),
               jnp.zeros((blocks, near_count, columns), jnp.float32), jnp.zeros((blocks, near_count, columns), jnp.float32),
               jnp.zeros((far_count, columns), jnp.float32), jnp.zeros((far_count, columns), jnp.float32))
    results = lax.fori_loop(0, columns // group_width, one_group, initial)
    attended_all, grad_query_all, near_gk, near_gv, far_gk, far_gv = results
    return (attended_all.reshape(tokens_here, columns), grad_query_all.reshape(tokens_here, columns),
            fold_back(near_gk, local_depth, tokens_here, columns), fold_back(near_gv, local_depth, tokens_here, columns),
            far_gk, far_gv)


def reference(query, key, value, grad_out, out_weight):
    total_depth = (TOKENS // POOL).bit_length() - 1
    local_depth = (TOK_DEV // POOL).bit_length() - 1
    seq_bits = total_depth - local_depth
    columns = HEADS * HEAD_DIM
    key_levels = build_levels(key, total_depth - 1)
    value_levels = build_levels(value, total_depth - 1)
    grad_in = jnp.dot(grad_out, out_weight.T, preferred_element_type=jnp.float32).astype(jnp.bfloat16)
    key_tables = [key_levels[local_depth + bit_index].reshape(N_SEQ >> bit_index, POOL, columns) for bit_index in range(seq_bits)]
    value_tables = [value_levels[local_depth + bit_index].reshape(N_SEQ >> bit_index, POOL, columns) for bit_index in range(seq_bits)]

    def visit_device(accumulated, device):
        def rows_of(levels, height_index):
            span = TOK_DEV >> height_index
            return lax.dynamic_slice_in_dim(levels[height_index], device * span, span, 0)

        siblings = [jnp.bitwise_xor(jnp.right_shift(device, bit_index), 1) for bit_index in range(seq_bits)]
        far_key = jnp.concatenate([lax.dynamic_index_in_dim(key_tables[bit_index], siblings[bit_index], 0, keepdims=False) for bit_index in range(seq_bits)], axis=0)
        far_value = jnp.concatenate([lax.dynamic_index_in_dim(value_tables[bit_index], siblings[bit_index], 0, keepdims=False) for bit_index in range(seq_bits)], axis=0)
        outputs = device_attention(rows_of([query], 0), [rows_of(key_levels, h_index) for h_index in range(local_depth)],
                                   [rows_of(value_levels, h_index) for h_index in range(local_depth)], rows_of([grad_in], 0), far_key, far_value)
        attended, grad_query, near_gk, near_gv, far_gk, far_gv = outputs
        key_acc, value_acc = accumulated
        key_acc = tuple(key_acc[bit_index].at[siblings[bit_index]].add(far_gk[bit_index * POOL:(bit_index + 1) * POOL]) for bit_index in range(seq_bits))
        value_acc = tuple(value_acc[bit_index].at[siblings[bit_index]].add(far_gv[bit_index * POOL:(bit_index + 1) * POOL]) for bit_index in range(seq_bits))
        return (key_acc, value_acc), (attended, grad_query, near_gk, near_gv)

    initial = (tuple(jnp.zeros((N_SEQ >> bit_index, POOL, columns), jnp.float32) for bit_index in range(seq_bits)),
               tuple(jnp.zeros((N_SEQ >> bit_index, POOL, columns), jnp.float32) for bit_index in range(seq_bits)))
    (key_acc, value_acc), stacked = lax.scan(visit_device, initial, jnp.arange(N_SEQ, dtype=jnp.int32))
    attended = stacked[0].reshape(TOKENS, columns)
    grad_query = stacked[1].reshape(TOKENS, columns)

    def descend(accs):
        running = None
        for bit_index in reversed(range(seq_bits)):
            term = accs[bit_index].reshape((N_SEQ >> bit_index) * POOL, columns)
            if running is not None:
                term = term + spread_pairs(running, 0)
            running = term
        for height_index in range(local_depth):
            running = spread_pairs(running, 0)
        return running

    grad_key = (stacked[2].reshape(TOKENS, columns) + descend(key_acc)).astype(jnp.bfloat16)
    grad_value = (stacked[3].reshape(TOKENS, columns) + descend(value_acc)).astype(jnp.bfloat16)
    mixed = jnp.dot(attended, out_weight, preferred_element_type=jnp.float32).astype(jnp.bfloat16)
    grad_weight = jnp.dot(attended.T, grad_out, preferred_element_type=jnp.float32) / TOKENS
    return mixed, grad_query, grad_key, grad_value, grad_weight
```

```python
import functools

import jax
import jax.numpy as jnp
from jax import lax
from jax.experimental import pallas as pl
from jax.experimental.pallas import tpu as pltpu
from jax.sharding import Mesh
from jax.sharding import PartitionSpec as P

HEAD_DIM = 64
POOL = 128
SEQ = ("seq_0", "seq_1", "seq_2")
MIB = 1 << 20
F32 = jnp.float32
BF16 = jnp.bfloat16

Z_PIECES = (("seq_2", 1, 128), ("seq_2", 2, 64), ("seq_2", 3, 64)) + tuple(
    ("seq_2", mask, 32) for mask in (4, 5, 6, 7)
)
Y_PIECES = (("seq_1", 1, 128), ("seq_1", 2, 64), ("seq_1", 3, 64))
X_PIECES = (("seq_0", 1, 128), ("seq_0", 2, 64), ("seq_0", 3, 64))


def from_partner(value, axis, mask):
    pairs = [(source, source ^ mask) for source in range(lax.axis_size(axis))]
    return lax.ppermute(value, axis, pairs)


def exchanged(values, pieces):
    return [from_partner(value, axis, mask) for value, (axis, mask, _) in zip(values, pieces)]


def whole(count):
    return [pl.BlockSpec(memory_space=pltpu.VMEM)] * count


def call(body, outs, *args, scratch=(), vmem=16, flops=0):
    return pl.pallas_call(
        body,
        out_shape=tuple(jax.ShapeDtypeStruct(shape, kind) for shape, kind in outs),
        in_specs=whole(len(args)),
        out_specs=tuple(whole(len(outs))),
        scratch_shapes=list(scratch),
        compiler_params=pltpu.CompilerParams(vmem_limit_bytes=vmem * MIB),
        cost_estimate=pl.CostEstimate(
            flops=flops, bytes_accessed=sum(a.size * a.dtype.itemsize for a in args), transcendentals=0
        ),
    )(*args)


def iotas(rows, columns):
    return (
        lax.broadcasted_iota(jnp.int32, (rows, columns), 0),
        lax.broadcasted_iota(jnp.int32, (rows, columns), 1),
    )


def halving(rows):
    row, column = iotas(rows, 2 * rows)
    return jnp.where(column // 2 == row, 0.5, 0.0).astype(BF16)


def halved(values):
    rows = values.shape[0] // 2
    return jnp.dot(halving(rows), values, preferred_element_type=F32).astype(BF16)


def spreading(rows, height):
    row, column = iotas(rows, rows >> height)
    return jnp.where((row >> height) == column, 2.0**-height, 0.0).astype(BF16)


def pool_body(key_ref, value_ref, one_ref, two_ref, three_ref):
    for at, ref in ((0, key_ref), (512, value_ref)):
        one = halved(ref[...])
        two = halved(one)
        one_ref[:, at : at + 512] = one
        two_ref[:, at : at + 512] = two
        three_ref[:, at : at + 512] = halved(two)


def climb_z_body(own, a, b, c, d, e, f, g, four_ref, five_ref):
    first = halved(halved(a[...]))
    rest = [halved(b[...]), halved(c[...])] + [r[...] for r in (d, e, f, g)]
    four = halved(jnp.concatenate([own[...], first] + rest, axis=0))
    four_ref[...] = four
    five_ref[...] = halved(four)


def climb_y_body(own, a, b, c, six_ref, seven_ref):
    six = halved(jnp.concatenate([own[...], halved(a[...]), b[...], c[...]], axis=0))
    six_ref[...] = six
    seven_ref[...] = halved(six)


def attention_body(*refs):
    query, key, value, grad = refs[:4]
    pieces = refs[4:17]
    attended_ref, grad_query_ref, near_ref = refs[17:20]
    far_refs = refs[20:33]
    listed = refs[33]
    tokens, columns = query.shape
    listed[:tokens, :columns] = key[...]
    listed[:tokens, columns:] = value[...]
    at = tokens
    for piece in pieces:
        rows = piece.shape[0]
        listed[at : at + rows] = piece[...]
        at += rows
    lane = lax.broadcasted_iota(jnp.int32, (tokens, 2 * HEAD_DIM), 1)
    first = lane < HEAD_DIM
    nt = (((1,), (1,)), ((), ()))
    tn = (((0,), (0,)), ((), ()))

    def by_head(block):
        zero = jnp.zeros_like(block)
        return jnp.concatenate([jnp.where(first, block, zero), jnp.where(first, zero, block)], axis=0)

    def own_halves(block):
        return jnp.where(first, block[:tokens], block[tokens:])

    for pair in range(columns // (2 * HEAD_DIM)):
        cut = slice(pair * 2 * HEAD_DIM, (pair + 1) * 2 * HEAD_DIM)
        cut_v = slice(columns + pair * 2 * HEAD_DIM, columns + (pair + 1) * 2 * HEAD_DIM)
        keys = listed[:, cut]
        values = listed[:, cut_v]
        queries = by_head(query[:, cut] * jnp.asarray(HEAD_DIM**-0.5, BF16))
        grads = by_head(grad[:, cut])
        scores = lax.dot_general(queries, keys, nt, preferred_element_type=F32)
        powers = jnp.exp(scores - jnp.max(scores, axis=1, keepdims=True))
        probs = powers * (1.0 / jnp.sum(powers, axis=1, keepdims=True))
        weights = probs.astype(BF16)
        grad_probs = lax.dot_general(grads, values, nt, preferred_element_type=F32)
        centred = jnp.sum(probs * grad_probs, axis=1, keepdims=True)
        grad_scores = (probs * (grad_probs - centred)).astype(BF16)
        attended_ref[:, cut] = own_halves(
            jnp.dot(weights, values, preferred_element_type=F32)
        ).astype(BF16)
        grad_query_ref[:, cut] = (
            own_halves(jnp.dot(grad_scores, keys, preferred_element_type=F32)) * HEAD_DIM**-0.5
        ).astype(BF16)
        for where, left, right in ((cut, grad_scores, queries), (cut_v, weights, grads)):
            total = lax.dot_general(left, right, tn, preferred_element_type=F32)
            near_ref[:, where] = total[:tokens]
            at = tokens
            for ref in far_refs:
                rows = ref.shape[0]
                ref[:, where] = total[at : at + rows].astype(BF16)
                at += rows


def down_x_body(own, two, three, four, a, b, c, carry_ref, two_ref, three_ref, four_ref):
    del own
    pairs = jnp.dot(spreading(128, 1), (b[...].astype(F32) + c[...].astype(F32)).astype(BF16), preferred_element_type=F32)
    six = a[...].astype(F32) + pairs
    for at, height, mine, ref in ((0, 2, None, carry_ref), (32, 2, two, two_ref), (64, 1, three, three_ref), (96, 1, four, four_ref)):
        part = six[at : at + 32].astype(BF16)
        out = jnp.dot(spreading(32 << height, height), part, preferred_element_type=F32)
        if mine is not None:
            out = out + mine[...].astype(F32)
        ref[...] = out.astype(BF16)


def down_y_body(*refs):
    mine = refs[:7]
    carry, a, b, c = refs[7:11]
    kept_ref = refs[11]
    outs = refs[12:19]
    pairs = jnp.dot(spreading(128, 1), (b[...].astype(F32) + c[...].astype(F32)).astype(BF16), preferred_element_type=F32)
    four = carry[...].astype(F32) + a[...].astype(F32) + pairs
    heights = (3, 2, 2, 1, 1, 1, 1)
    kept_ref[...] = four[:16].astype(BF16)
    for index, (height, own, ref) in enumerate(zip(heights, mine, outs)):
        part = four[16 * (index + 1) : 16 * (index + 2)].astype(BF16)
        out = jnp.dot(spreading(16 << height, height), part, preferred_element_type=F32)
        ref[...] = (out + own[...].astype(F32)).astype(BF16)


def down_z_body(near, kept, a, b, c, d, e, f, g, key_ref, value_ref):
    total = near[...]
    total = total + jnp.dot(spreading(256, 4), kept[...], preferred_element_type=F32)
    total = total + jnp.dot(spreading(256, 1), a[...], preferred_element_type=F32)
    for ref in (b, c):
        total = total + jnp.dot(spreading(256, 2), ref[...], preferred_element_type=F32)
    for ref in (d, e, f, g):
        total = total + jnp.dot(spreading(256, 3), ref[...], preferred_element_type=F32)
    key_ref[...] = total[:, :512].astype(BF16)
    value_ref[...] = total[:, 512:].astype(BF16)


def summed_parts(value, axis):
    size = lax.axis_size(axis)
    blocks = value.astype(BF16).reshape(size, value.shape[0] // size, value.shape[1])
    arrived = lax.all_to_all(blocks, axis, 0, 0, tiled=True)
    return jnp.sum(arrived.astype(F32), axis=0)


def gathered_parts(value, axis):
    size = lax.axis_size(axis)
    blocks = lax.all_to_all(jnp.broadcast_to(value[None], (size, *value.shape)), axis, 0, 0, tiled=True)
    return blocks.reshape(size * value.shape[0], value.shape[1])


def per_device(query, key, value, grad_out, out_weight):
    tokens_here, columns = query.shape
    width = 2 * columns
    seq_count = lax.axis_size(SEQ)
    head = lax.axis_index("head")
    one, two, three = call(
        pool_body, [((128, width), BF16), ((64, width), BF16), ((32, width), BF16)], key, value
    )
    from_z = exchanged((one, two, two, three, three, three, three), Z_PIECES)
    other_grad = from_partner(grad_out, "head", 1)
    other_rows = from_partner(
        lax.dynamic_slice_in_dim(out_weight, (1 - head) * columns, columns, 1), "head", 1
    )
    own_rows = lax.dynamic_slice_in_dim(out_weight, head * columns, columns, 1)
    first = head == 0
    full_grad = jnp.concatenate(
        (jnp.where(first, grad_out, other_grad), jnp.where(first, other_grad, grad_out)), axis=1
    )
    grad_in = jnp.einsum("td,cd->tc", full_grad, out_weight, preferred_element_type=F32).astype(BF16)
    four, five = call(climb_z_body, [((128, width), BF16), ((64, width), BF16)], three, *from_z)
    from_y = exchanged((four, five, five), Y_PIECES)
    six, seven = call(climb_y_body, [((128, width), BF16), ((64, width), BF16)], five, *from_y)
    from_x = exchanged((six, seven, seven), X_PIECES)
    pieces = Z_PIECES + Y_PIECES + X_PIECES
    results = call(
        attention_body,
        [((tokens_here, columns), BF16), ((tokens_here, columns), BF16), ((tokens_here, width), F32)]
        + [((rows, width), BF16) for _, _, rows in pieces],
        query, key, value, grad_in, *from_z, *from_y, *from_x,
        scratch=[pltpu.VMEM((tokens_here + 7 * POOL, width), BF16)],
        vmem=48,
    )
    attended, grad_query, near = results[:3]
    far_z, far_y, far_x = results[3:10], results[10:13], results[13:16]
    back_x = exchanged(far_x, X_PIECES)
    carry, *to_y = call(
        down_x_body,
        [((128, width), BF16), ((128, width), BF16), ((64, width), BF16), ((64, width), BF16)],
        far_y[0], *far_y, *back_x,
    )
    back_y = exchanged(to_y, Y_PIECES)
    kept, *to_z = call(
        down_y_body,
        [((16, width), BF16)] + [((rows, width), BF16) for _, _, rows in Z_PIECES],
        *far_z, carry, *back_y,
    )
    back_z = exchanged(to_z, Z_PIECES)
    grad_key, grad_value = call(
        down_z_body,
        [((tokens_here, columns), BF16), ((tokens_here, columns), BF16)],
        near, kept, *back_z,
    )
    other_attended = from_partner(attended, "head", 1)
    mixed = (
        jnp.dot(attended, own_rows, preferred_element_type=F32)
        + jnp.dot(other_attended, other_rows, preferred_element_type=F32)
    ).astype(BF16)
    term = jnp.einsum("tc,td->cd", attended, full_grad, preferred_element_type=F32) / (
        tokens_here * seq_count
    )
    for axis in SEQ:
        term = summed_parts(term, axis)
    grad_weight = term.astype(BF16)
    for axis in reversed(SEQ):
        grad_weight = gathered_parts(grad_weight, axis)
    return mixed, grad_query, grad_key, grad_value, grad_weight.astype(F32)


def solution(mesh):
    finer = Mesh(
        mesh.devices.reshape(4, 4, 8, mesh.shape["head"]), ("seq_0", "seq_1", "seq_2", "head")
    )
    in_specs = (P(SEQ, "head"), P(SEQ, "head"), P(SEQ, "head"), P(SEQ, "head"), P("head", None))
    out_specs = (P(SEQ, "head"), P(SEQ, "head"), P(SEQ, "head"), P(SEQ, "head"), P("head", None))
    return jax.shard_map(
        per_device, mesh=finer, in_specs=in_specs, out_specs=out_specs, check_vma=False
    )
```

```python
import jax
import jax.numpy as jnp
from jax import lax
from jax.experimental import pallas as pl
from jax.experimental.pallas import tpu as pltpu
from jax.sharding import Mesh
from jax.sharding import PartitionSpec as P

HEAD_DIM = 64
POOL = 128
X, Y, Z = "seq_0", "seq_1", "seq_2"
SEQ = (X, Y, Z)
MIB = 1 << 20
F32 = jnp.float32
BF16 = jnp.bfloat16


def from_partner(value, axis, mask):
    pairs = [(source, source ^ mask) for source in range(lax.axis_size(axis))]
    return lax.ppermute(value, axis, pairs)


def to_others(values, axis, masks):
    return [from_partner(value, axis, mask) for value, mask in zip(values, masks)]


def call(body, outs, *args, scratch=(), vmem=4, after=()):
    def ordered(*refs):
        body(*refs[: len(args)], *refs[len(args) + len(after) :])

    whole = pl.BlockSpec(memory_space=pltpu.VMEM)
    return pl.pallas_call(
        ordered,
        out_shape=tuple(jax.ShapeDtypeStruct(shape, kind) for shape, kind in outs),
        in_specs=[whole] * len(args) + [pl.BlockSpec(memory_space=pl.ANY)] * len(after),
        out_specs=(whole,) * len(outs),
        scratch_shapes=list(scratch),
        compiler_params=pltpu.CompilerParams(vmem_limit_bytes=vmem * MIB),
    )(*args, *after)


def iotas(rows, columns):
    return (
        lax.broadcasted_iota(jnp.int32, (rows, columns), 0),
        lax.broadcasted_iota(jnp.int32, (rows, columns), 1),
    )


def halved(values):
    rows = values.shape[0] // 2
    row, column = iotas(rows, 2 * rows)
    means = jnp.where((column >> 1) == row, 0.5, 0.0).astype(BF16)
    return jnp.dot(means, values, preferred_element_type=F32).astype(BF16)


def spread(values, height):
    values = values.astype(BF16)
    rows = values.shape[0] << height
    row, column = iotas(rows, values.shape[0])
    shares = jnp.where((row >> height) == column, 2.0**-height, 0.0).astype(BF16)
    return jnp.dot(shares, values, preferred_element_type=F32)


def wide(ref, start=0, rows=None):
    rows = ref.shape[0] - start if rows is None else rows
    return ref[start : start + rows].astype(F32)


def pool_body(key_ref, value_ref, one_ref, two_ref, three_ref):
    columns = key_ref.shape[1]
    for at, ref in ((0, key_ref), (columns, value_ref)):
        one = halved(ref[...])
        two = halved(one)
        one_ref[:, at : at + columns] = one
        two_ref[:, at : at + columns] = two
        three_ref[:, at : at + columns] = halved(two)


def pair_body(three, from_1, two_ref, pair_ref):
    two = halved(from_1[...])
    two_ref[...] = two
    pair_ref[:32] = three[...]
    pair_ref[32:] = halved(two)


def climb_z_body(pair, from_3, beside_3, from_5, from_7, four_ref, five_ref):
    rows = [pair[...], halved(from_3[...]), halved(beside_3[...]), from_5[...], from_7[...]]
    four = halved(jnp.concatenate(rows, axis=0))
    four_ref[...] = four
    five_ref[...] = halved(four)


def climb_y_body(five, from_1, from_2, from_3, six_ref, seven_ref):
    rows = [five[...], halved(from_1[...]), from_2[...], from_3[...]]
    six = halved(jnp.concatenate(rows, axis=0))
    six_ref[...] = six
    seven_ref[...] = halved(six)


def attention_body(*refs):
    query, key, value, grad = refs[:4]
    pieces = refs[4:15]
    attended_ref, grad_query_ref, near_ref = refs[15:18]
    far_refs = refs[18:23]
    listed = refs[23]
    tokens, columns = query.shape
    listed[:tokens, :columns] = key[...]
    listed[:tokens, columns:] = value[...]
    at = tokens
    for piece in pieces:
        rows = piece.shape[0]
        listed[at : at + rows] = piece[...]
        at += rows
    lane = lax.broadcasted_iota(jnp.int32, (tokens, 2 * HEAD_DIM), 1)
    first = lane < HEAD_DIM
    nt = (((1,), (1,)), ((), ()))
    tn = (((0,), (0,)), ((), ()))

    def by_head(block):
        zero = jnp.zeros_like(block)
        return jnp.concatenate([jnp.where(first, block, zero), jnp.where(first, zero, block)], axis=0)

    def own_halves(block):
        return jnp.where(first, block[:tokens], block[tokens:])

    for pair in range(columns // (2 * HEAD_DIM)):
        cut = slice(pair * 2 * HEAD_DIM, (pair + 1) * 2 * HEAD_DIM)
        cut_v = slice(columns + pair * 2 * HEAD_DIM, columns + (pair + 1) * 2 * HEAD_DIM)
        keys = listed[:, cut]
        values = listed[:, cut_v]
        queries = by_head(query[:, cut] * jnp.asarray(HEAD_DIM**-0.5, BF16))
        grads = by_head(grad[:, cut])
        scores = lax.dot_general(queries, keys, nt, preferred_element_type=F32)
        powers = jnp.exp(scores - jnp.max(scores, axis=1, keepdims=True))
        probs = powers * (1.0 / jnp.sum(powers, axis=1, keepdims=True))
        weights = probs.astype(BF16)
        grad_probs = lax.dot_general(grads, values, nt, preferred_element_type=F32)
        centred = jnp.sum(probs * grad_probs, axis=1, keepdims=True)
        grad_scores = (probs * (grad_probs - centred)).astype(BF16)
        attended_ref[:, cut] = own_halves(
            jnp.dot(weights, values, preferred_element_type=F32)
        ).astype(BF16)
        grad_query_ref[:, cut] = (
            own_halves(jnp.dot(grad_scores, keys, preferred_element_type=F32)) * HEAD_DIM**-0.5
        ).astype(BF16)
        for where, left, right in ((cut, grad_scores, queries), (cut_v, weights, grads)):
            total = lax.dot_general(left, right, tn, preferred_element_type=F32)
            near_ref[:, where] = total[:tokens]
            at = tokens
            for ref in far_refs:
                rows = ref.shape[0]
                ref[:, where] = total[at : at + rows].astype(BF16)
                at += rows


def down_x_body(mine, back_1, back_2, back_3, carry_ref, one_ref, two_ref, three_ref):
    six = wide(back_1) + spread(wide(back_2) + wide(back_3), 1)
    carry_ref[...] = spread(six[:32], 2).astype(BF16)
    one_ref[...] = (wide(mine, 0, 128) + spread(six[32:64], 2)).astype(BF16)
    two_ref[...] = (wide(mine, 128, 64) + spread(six[64:96], 1)).astype(BF16)
    three_ref[...] = (wide(mine, 192, 64) + spread(six[96:], 1)).astype(BF16)


def down_y_body(mine, carry, back_1, back_2, back_3, four_ref, beside_ref, five_ref, seven_ref):
    four = wide(carry) + wide(back_1) + spread(wide(back_2) + wide(back_3), 1)
    four_ref[...] = four.astype(BF16)
    beside_ref[...] = (wide(mine, 192, 64) + spread(four[48:64], 2)).astype(BF16)
    five_ref[...] = (wide(mine, 256, 64) + spread(four[64:96], 1)).astype(BF16)
    seven_ref[...] = (wide(mine, 320, 64) + spread(four[96:], 1)).astype(BF16)


def down_pair_body(mine, four, beside, back_5, back_7, one_ref, three_ref):
    total = wide(mine, 0, 128) + spread(wide(four, 16, 16), 3) + spread(beside[...], 1)
    total = total + spread(wide(back_5, 32, 32) + wide(back_7, 32, 32), 2)
    one_ref[...] = total.astype(BF16)
    three_ref[...] = (wide(mine, 128, 64) + spread(wide(four, 32, 16), 2)).astype(BF16)


def down_z_body(near, four, back_5, back_7, back_1, back_3, key_ref, value_ref):
    columns = key_ref.shape[1]
    total = near[...] + spread(wide(four, 0, 16), 4) + spread(back_1[...], 1) + spread(back_3[...], 2)
    total = total + spread(wide(back_5, 0, 32) + wide(back_7, 0, 32), 3)
    key_ref[...] = total[:, :columns].astype(BF16)
    value_ref[...] = total[:, columns:].astype(BF16)


def quarters_body(own, other, *out_refs):
    me = lax.axis_index(Y)
    for mask, ref in enumerate(out_refs):
        cut = cut_at(me ^ mask, POOL)
        ref[:, :POOL] = own[:, cut]
        ref[:, POOL:] = other[:, cut]


def weight_body(*refs):
    lefts, rights, own_ref, other_ref = refs[:4], refs[4:8], refs[8], refs[9]
    total = None
    for left, right in zip(lefts, rights):
        part = lax.dot_general(
            left[...], right[...], (((0,), (0,)), ((), ())), preferred_element_type=F32
        )
        total = part if total is None else total + part
    total = (total * (1.0 / 32768)).astype(BF16)
    own_ref[...] = total[:POOL]
    other_ref[...] = total[POOL:]


def blocks_body(own, other, *out_refs):
    columns = own.shape[1]
    me, head = lax.axis_index(X), lax.axis_index("head")
    for mask, ref in enumerate(out_refs):
        rows = pl.ds(pl.multiple_of((me ^ mask) * 32, 32), 32)
        ref[:, cut_at(head, columns)] = own[rows]
        ref[:, cut_at(1 - head, columns)] = other[rows]


def sum_body(*refs):
    total = wide(refs[0])
    for ref in refs[1:-1]:
        total = total + wide(ref)
    refs[-1][...] = total.astype(BF16)


def join_body(*refs):
    me = lax.axis_index(X)
    out_ref = refs[4]
    for mask, ref in enumerate(refs[:4]):
        out_ref[pl.ds(pl.multiple_of((me ^ mask) * 32, 32), 32)] = ref[...]


def widen_body(*refs):
    me = lax.axis_index(Y)
    out_ref = refs[4]
    for mask, ref in enumerate(refs[:4]):
        out_ref[cut_at(me ^ mask, POOL)] = wide(ref)


def cut_at(side, columns):
    return pl.ds(pl.multiple_of(side * columns, columns), columns)


def columns_body(weight, out_ref):
    columns = out_ref.shape[1]
    out_ref[...] = weight[:, cut_at(1 - lax.axis_index("head"), columns)]


def grad_in_body(own, other, weight, out_ref):
    columns = own.shape[1]
    head = lax.axis_index("head")
    nt = (((1,), (1,)), ((), ()))
    total = lax.dot_general(own[...], weight[:, cut_at(head, columns)], nt, preferred_element_type=F32)
    total = total + lax.dot_general(
        other[...], weight[:, cut_at(1 - head, columns)], nt, preferred_element_type=F32
    )
    out_ref[...] = total.astype(BF16)


def mixed_body(own, other, weight, other_rows, out_ref):
    columns = own.shape[1]
    own_rows = weight[:, cut_at(lax.axis_index("head"), columns)]
    total = jnp.dot(own[...], own_rows, preferred_element_type=F32)
    total = total + jnp.dot(other[...], other_rows[...], preferred_element_type=F32)
    out_ref[...] = total.astype(BF16)


def per_device(query, key, value, grad_out, out_weight):
    tokens, columns = query.shape
    width = 2 * columns

    def rows(*counts):
        return [((count, width), BF16) for count in counts]

    one, two, three = call(pool_body, rows(128, 64, 32), key, value)
    z_1 = from_partner(one, Z, 1)
    z_3 = from_partner(two, Z, 3)
    grads = [grad_out] + to_others([grad_out] * 3, Y, (1, 2, 3))
    two, pair = call(pair_body, rows(64, 64), three, z_1)
    beside_3, z_5, z_7 = to_others((two, pair, pair), Z, (3, 5, 7))
    four, five = call(climb_z_body, rows(128, 64), pair, z_3, beside_3, z_5, z_7)
    other_grad = from_partner(grad_out, "head", 1)
    (other_rows,) = call(columns_body, [((columns, columns), BF16)], out_weight)
    other_rows = from_partner(other_rows, "head", 1)
    (grad_in,) = call(grad_in_body, [((tokens, columns), BF16)], grad_out, other_grad, out_weight)
    y_1, y_2, y_3 = to_others((four, five, five), Y, (1, 2, 3))
    six, seven = call(climb_y_body, rows(128, 64), five, y_1, y_2, y_3)
    x_1, x_2, x_3 = to_others((six, seven, seven), X, (1, 2, 3))
    attended, grad_query, near, far_x_1, far_x_2, far_x_3, far_y, far_z = call(
        attention_body,
        [((tokens, columns), BF16), ((tokens, columns), BF16), ((tokens, width), F32)]
        + rows(128, 64, 64, 256, 384),
        query, key, value, grad_in, x_1, x_2, x_3, y_1, y_2, y_3, z_1, z_3, beside_3, z_5, z_7,
        scratch=[pltpu.VMEM((tokens + 7 * POOL, width), BF16)],
        vmem=16,
        after=(other_rows, *grads[1:]),
    )
    back_x = to_others((far_x_1, far_x_2, far_x_3), X, (1, 2, 3))
    other_attended = from_partner(attended, "head", 1)
    quarters = call(quarters_body, [((tokens, 2 * POOL), BF16)] * 4, attended, other_attended)
    quarters = [quarters[0]] + to_others(quarters[1:], Y, (1, 2, 3))
    carry, *to_y = call(down_x_body, rows(128, 128, 64, 64), far_y, *back_x)
    back_y = to_others(to_y, Y, (1, 2, 3))
    own_term, term = call(
        weight_body, [((POOL, columns), BF16)] * 2, *quarters, *grads, after=(carry,)
    )
    term = from_partner(term, "head", 1)
    terms = call(blocks_body, rows(32, 32, 32, 32), own_term, term)
    terms = [terms[0]] + to_others(terms[1:], X, (1, 2, 3))
    (term,) = call(sum_body, rows(32), *terms)
    four, beside, to_5, to_7 = call(down_y_body, rows(128, 64, 64, 64), far_z, carry, *back_y)
    beside, back_5, back_7 = to_others((beside, to_5, to_7), Z, (3, 5, 7))
    (term,) = call(sum_body, rows(32), term, *to_others([term] * 3, Z, (3, 5, 6)))
    (term,) = call(sum_body, rows(32), term, from_partner(term, Z, 1))
    (term,) = call(join_body, rows(128), term, *to_others([term] * 3, X, (1, 2, 3)))
    to_1, to_3 = call(down_pair_body, rows(128, 64), far_z, four, beside, back_5, back_7)
    back_1, back_3 = to_others((to_1, to_3), Z, (1, 3))
    others = to_others([term] * 3, Y, (1, 2, 3))
    (mixed,) = call(
        mixed_body, [((tokens, columns), BF16)], attended, other_attended, out_weight, other_rows, after=(four,)
    )
    grad_key, grad_value = call(
        down_z_body, [((tokens, columns), BF16)] * 2, near, four, back_5, back_7, back_1, back_3
    )
    (grad_weight,) = call(widen_body, [((columns, width), F32)], term, *others, vmem=6)
    return mixed, grad_query, grad_key, grad_value, grad_weight


def solution(mesh):
    finer = Mesh(mesh.devices.reshape(4, 4, 8, mesh.shape["head"]), (*SEQ, "head"))
    in_specs = (P(SEQ, "head"), P(SEQ, "head"), P(SEQ, "head"), P(SEQ, "head"), P("head", None))
    return jax.shard_map(
        per_device, mesh=finer, in_specs=in_specs, out_specs=in_specs, check_vma=False
    )
```

```python
import jax
import jax.numpy as jnp
from jax import lax
from jax.experimental import pallas as pl
from jax.experimental.pallas import tpu as pltpu
from jax.sharding import Mesh
from jax.sharding import PartitionSpec as P

HEAD_DIM = 64
POOL = 128
X, Y, Z = "seq_0", "seq_1", "seq_2"
SEQ = (X, Y, Z)
MIB = 1 << 20
F32 = jnp.float32
BF16 = jnp.bfloat16


def from_partner(value, axis, mask):
    pairs = [(source, source ^ mask) for source in range(lax.axis_size(axis))]
    return lax.ppermute(value, axis, pairs)


def to_others(values, axis, masks):
    return [from_partner(value, axis, mask) for value, mask in zip(values, masks)]


def call(body, outs, *args, scratch=(), vmem=4, after=(), through=(), flops=0):
    count, passed = len(args), len(after) + len(through)

    def ordered(*refs):
        made = refs[count + passed :]
        body(*refs[:count], *made[: len(outs)], *made[len(outs) + len(through) :])

    whole, anywhere = pl.BlockSpec(memory_space=pltpu.VMEM), pl.BlockSpec(memory_space=pl.ANY)
    return pl.pallas_call(
        ordered,
        out_shape=tuple(jax.ShapeDtypeStruct(shape, kind) for shape, kind in outs)
        + tuple(jax.ShapeDtypeStruct(value.shape, value.dtype) for value in through),
        in_specs=[whole] * count + [anywhere] * passed,
        out_specs=(whole,) * len(outs) + (anywhere,) * len(through),
        scratch_shapes=list(scratch),
        input_output_aliases={count + len(after) + at: len(outs) + at for at in range(len(through))},
        compiler_params=pltpu.CompilerParams(vmem_limit_bytes=vmem * MIB),
        cost_estimate=pl.CostEstimate(flops=flops, bytes_accessed=0, transcendentals=0) if flops else None,
    )(*args, *after, *through)


def iotas(rows, columns):
    return (
        lax.broadcasted_iota(jnp.int32, (rows, columns), 0),
        lax.broadcasted_iota(jnp.int32, (rows, columns), 1),
    )


def halved(values):
    rows = values.shape[0] // 2
    row, column = iotas(rows, 2 * rows)
    means = jnp.where((column >> 1) == row, 0.5, 0.0).astype(BF16)
    return jnp.dot(means, values, preferred_element_type=F32).astype(BF16)


def spread(values, height):
    values = values.astype(BF16)
    rows = values.shape[0] << height
    row, column = iotas(rows, values.shape[0])
    shares = jnp.where((row >> height) == column, 2.0**-height, 0.0).astype(BF16)
    return jnp.dot(shares, values, preferred_element_type=F32)


def wide(ref, start=0, rows=None):
    rows = ref.shape[0] - start if rows is None else rows
    return ref[start : start + rows].astype(F32)


def cut_at(side, columns):
    return pl.ds(pl.multiple_of(side * columns, columns), columns)


def pool_body(key_ref, value_ref, one_ref, two_ref, three_ref):
    columns = key_ref.shape[1]
    for at, ref in ((0, key_ref), (columns, value_ref)):
        one = halved(ref[...])
        two = halved(one)
        one_ref[:, at : at + columns] = one
        two_ref[:, at : at + columns] = two
        three_ref[:, at : at + columns] = halved(two)


def pair_body(three, from_1, two_ref, pair_ref):
    two = halved(from_1[...])
    two_ref[...] = two
    pair_ref[:32] = three[...]
    pair_ref[32:] = halved(two)


def climb_z_body(pair, from_3, beside_3, from_5, from_7, four_ref, five_ref):
    rows = [pair[...], halved(from_3[...]), halved(beside_3[...]), from_5[...], from_7[...]]
    four = halved(jnp.concatenate(rows, axis=0))
    four_ref[...] = four
    five_ref[...] = halved(four)


def climb_y_body(five, from_1, from_2, from_3, six_ref, seven_ref):
    rows = [five[...], halved(from_1[...]), from_2[...], from_3[...]]
    six = halved(jnp.concatenate(rows, axis=0))
    six_ref[...] = six
    seven_ref[...] = halved(six)


PAIR = 2 * HEAD_DIM
NT = (((1,), (1,)), ((), ()))
TN = (((0,), (0,)), ((), ()))


def first_head(rows):
    return lax.broadcasted_iota(jnp.int32, (rows, PAIR), 1) < HEAD_DIM


def by_head(block):
    first, zero = first_head(block.shape[0]), jnp.zeros_like(block)
    return jnp.concatenate([jnp.where(first, block, zero), jnp.where(first, zero, block)], axis=0)


def side_by_side(block):
    rows = block.shape[0] // 2
    return jnp.where(first_head(rows), block[:rows], block[rows:])


def scaled(block):
    return block * jnp.asarray(HEAD_DIM**-0.5, BF16)


def forward_body(*refs):
    query, key, value = refs[:3]
    pieces = refs[3:14]
    attended_ref, probs_ref, listed = refs[14:17]
    quarter_refs = refs[17:21]
    tokens, columns = query.shape
    listed[:tokens, :columns] = key[...]
    listed[:tokens, columns:] = value[...]
    at = tokens
    for piece in pieces:
        rows = piece.shape[0]
        listed[at : at + rows] = piece[...]
        at += rows
    for pair in range(columns // PAIR):
        cut = slice(pair * PAIR, (pair + 1) * PAIR)
        cut_v = slice(columns + pair * PAIR, columns + (pair + 1) * PAIR)
        queries = by_head(scaled(query[:, cut]))
        scores = lax.dot_general(queries, listed[:, cut], NT, preferred_element_type=F32)
        powers = jnp.exp(scores - jnp.max(scores, axis=1, keepdims=True))
        probs = powers * (1.0 / jnp.sum(powers, axis=1, keepdims=True))
        probs_ref[pair] = probs
        attended_ref[:, cut] = side_by_side(
            jnp.dot(probs.astype(BF16), listed[:, cut_v], preferred_element_type=F32)
        ).astype(BF16)
    me = lax.axis_index(X)
    for mask, ref in enumerate(quarter_refs):
        ref[...] = attended_ref[:, cut_at(me ^ mask, POOL)]


def backward_body(*refs):
    query, grad, listed, probs_ref = refs[:4]
    grad_query_ref, near_ref = refs[4:6]
    far_refs = refs[6:]
    tokens, columns = query.shape
    for pair in range(columns // PAIR):
        cut = slice(pair * PAIR, (pair + 1) * PAIR)
        cut_v = slice(columns + pair * PAIR, columns + (pair + 1) * PAIR)
        keys, values = listed[:, cut], listed[:, cut_v]
        queries = by_head(scaled(query[:, cut]))
        grads = by_head(grad[:, cut])
        probs = probs_ref[pair]
        weights = probs.astype(BF16)
        grad_probs = lax.dot_general(grads, values, NT, preferred_element_type=F32)
        centred = jnp.sum(probs * grad_probs, axis=1, keepdims=True)
        grad_scores = (probs * (grad_probs - centred)).astype(BF16)
        grad_query_ref[:, cut] = (
            side_by_side(jnp.dot(grad_scores, keys, preferred_element_type=F32)) * HEAD_DIM**-0.5
        ).astype(BF16)
        for where, left, right in ((cut, grad_scores, queries), (cut_v, weights, grads)):
            total = lax.dot_general(left, right, TN, preferred_element_type=F32)
            near_ref[:, where] = total[:tokens]
            at = tokens
            for ref in far_refs:
                rows = ref.shape[0]
                ref[:, where] = total[at : at + rows].astype(BF16)
                at += rows


def down_x_body(mine, back_1, back_2, back_3, carry_ref, one_ref, two_ref, three_ref):
    six = wide(back_1) + spread(wide(back_2) + wide(back_3), 1)
    carry_ref[...] = spread(six[:32], 2).astype(BF16)
    one_ref[...] = (wide(mine, 0, 128) + spread(six[32:64], 2)).astype(BF16)
    two_ref[...] = (wide(mine, 128, 64) + spread(six[64:96], 1)).astype(BF16)
    three_ref[...] = (wide(mine, 192, 64) + spread(six[96:], 1)).astype(BF16)


def down_y_body(mine, carry, back_1, back_2, back_3, four_ref, beside_ref, five_ref, seven_ref):
    four = wide(carry) + wide(back_1) + spread(wide(back_2) + wide(back_3), 1)
    four_ref[...] = four.astype(BF16)
    beside_ref[...] = (wide(mine, 192, 64) + spread(four[48:64], 2)).astype(BF16)
    five_ref[...] = (wide(mine, 256, 64) + spread(four[64:96], 1)).astype(BF16)
    seven_ref[...] = (wide(mine, 320, 64) + spread(four[96:], 1)).astype(BF16)


def down_pair_body(mine, four, beside, back_5, back_7, one_ref, three_ref):
    total = wide(mine, 0, 128) + spread(wide(four, 16, 16), 3) + spread(beside[...], 1)
    total = total + spread(wide(back_5, 32, 32) + wide(back_7, 32, 32), 2)
    one_ref[...] = total.astype(BF16)
    three_ref[...] = (wide(mine, 128, 64) + spread(wide(four, 32, 16), 2)).astype(BF16)


def down_z_body(near, four, back_5, back_7, back_1, back_3, key_ref, value_ref):
    columns = key_ref.shape[1]
    total = near[...] + spread(wide(four, 0, 16), 4) + spread(back_1[...], 1) + spread(back_3[...], 2)
    total = total + spread(wide(back_5, 0, 32) + wide(back_7, 0, 32), 3)
    key_ref[...] = total[:, :columns].astype(BF16)
    value_ref[...] = total[:, columns:].astype(BF16)


def weight_body(*refs):
    lefts, own_grads, other_grads, out_refs, total_ref = refs[:4], refs[4:8], refs[8:12], refs[12:16], refs[16]
    columns = own_grads[0].shape[1]
    me, head = lax.axis_index(Y), lax.axis_index("head")
    for side, rights in ((head, own_grads), (1 - head, other_grads)):
        total = None
        for left, right in zip(lefts, rights):
            part = lax.dot_general(left[...], right[...], TN, preferred_element_type=F32)
            total = part if total is None else total + part
        total_ref[:, cut_at(side, columns)] = total * (1.0 / 32768)
    for mask, ref in enumerate(out_refs):
        ref[...] = total_ref[pl.ds(pl.multiple_of((me ^ mask) * 32, 32), 32)].astype(BF16)


def sum_body(*refs):
    total = wide(refs[0])
    for ref in refs[1:-1]:
        total = total + wide(ref)
    refs[-1][...] = total.astype(BF16)


def join_body(*refs):
    me = lax.axis_index(Y)
    out_ref = refs[4]
    for mask, ref in enumerate(refs[:4]):
        out_ref[pl.ds(pl.multiple_of((me ^ mask) * 32, 32), 32)] = ref[...]


def widen_body(*refs):
    me = lax.axis_index(X)
    out_ref = refs[4]
    for mask, ref in enumerate(refs[:4]):
        out_ref[cut_at(me ^ mask, POOL)] = wide(ref)


def columns_body(weight, out_ref):
    columns = out_ref.shape[1]
    out_ref[...] = weight[:, cut_at(1 - lax.axis_index("head"), columns)]


def grad_in_body(own, other, weight, out_ref):
    columns = own.shape[1]
    head = lax.axis_index("head")
    nt = (((1,), (1,)), ((), ()))
    total = lax.dot_general(own[...], weight[:, cut_at(head, columns)], nt, preferred_element_type=F32)
    total = total + lax.dot_general(
        other[...], weight[:, cut_at(1 - head, columns)], nt, preferred_element_type=F32
    )
    out_ref[...] = total.astype(BF16)


def mixed_body(own, other, weight, other_rows, out_ref):
    columns = own.shape[1]
    own_rows = weight[:, cut_at(lax.axis_index("head"), columns)]
    total = jnp.dot(own[...], own_rows, preferred_element_type=F32)
    total = total + jnp.dot(other[...], other_rows[...], preferred_element_type=F32)
    out_ref[...] = total.astype(BF16)


def per_device(query, key, value, grad_out, out_weight):
    tokens, columns = query.shape
    width = 2 * columns

    def rows(*counts):
        return [((count, width), BF16) for count in counts]

    one, two, three = call(pool_body, rows(128, 64, 32), key, value)
    z_1 = from_partner(one, Z, 1)
    z_3 = from_partner(two, Z, 3)
    grads = [grad_out] + to_others([grad_out] * 3, X, (1, 2, 3))
    two, pair = call(pair_body, rows(64, 64), three, z_1)
    beside_3, z_5, z_7 = to_others((two, pair, pair), Z, (3, 5, 7))
    four, five = call(climb_z_body, rows(128, 64), pair, z_3, beside_3, z_5, z_7, after=grads[1:])
    y_1, y_2, y_3 = to_others((four, five, five), Y, (1, 2, 3))
    other_grads = [from_partner(grad, "head", 1) for grad in grads]
    (other_rows,) = call(columns_body, [((columns, columns), BF16)], out_weight)
    other_rows = from_partner(other_rows, "head", 1)
    (grad_in,) = call(grad_in_body, [((tokens, columns), BF16)], grad_out, other_grads[0], out_weight)
    six, seven = call(climb_y_body, rows(128, 64), five, y_1, y_2, y_3)
    x_1, x_2, x_3 = to_others((six, seven, seven), X, (1, 2, 3))
    listed_rows = tokens + 7 * POOL
    attended, probs, listed, *quarters = call(
        forward_body,
        [((tokens, columns), BF16), ((columns // PAIR, 2 * tokens, listed_rows), F32), ((listed_rows, width), BF16)]
        + [((tokens, POOL), BF16)] * 4,
        query, key, value, x_1, x_2, x_3, y_1, y_2, y_3, z_1, z_3, beside_3, z_5, z_7,
        vmem=12,
        flops=6 * 10**9,
        after=(other_rows, *other_grads),
    )
    quarters = [quarters[0]] + to_others(quarters[1:], X, (1, 2, 3))
    grad_query, near, far_x_1, far_x_2, far_x_3, far_y, far_z = call(
        backward_body,
        [((tokens, columns), BF16), ((tokens, width), F32)] + rows(128, 64, 64, 256, 384),
        query, grad_in, listed, probs,
        vmem=16,
        flops=8 * 10**9,
    )
    *terms, far_x_1, far_x_2, far_x_3 = call(
        weight_body, rows(32, 32, 32, 32), *quarters, *grads, *other_grads,
        scratch=[pltpu.VMEM((POOL, width), F32)],
        through=(far_x_1, far_x_2, far_x_3),
    )
    back_x = to_others((far_x_1, far_x_2, far_x_3), X, (1, 2, 3))
    terms = [terms[0]] + to_others(terms[1:], Y, (1, 2, 3))
    carry, *to_y = call(down_x_body, rows(128, 128, 64, 64), far_y, *back_x)
    back_y = to_others(to_y, Y, (1, 2, 3))
    other_attended = from_partner(attended, "head", 1)
    (term,) = call(sum_body, rows(32), *terms)
    four, beside, to_5, to_7 = call(down_y_body, rows(128, 64, 64, 64), far_z, carry, *back_y)
    beside, back_5, back_7 = to_others((beside, to_5, to_7), Z, (3, 5, 7))
    (term,) = call(sum_body, rows(32), term, *to_others([term] * 3, Z, (3, 5, 6)))
    (term,) = call(sum_body, rows(32), term, from_partner(term, Z, 1))
    (term,) = call(join_body, rows(128), term, *to_others([term] * 3, Y, (1, 2, 3)))
    to_1, to_3 = call(down_pair_body, rows(128, 64), far_z, four, beside, back_5, back_7)
    back_1, back_3 = to_others((to_1, to_3), Z, (1, 3))
    others = to_others([term] * 3, X, (1, 2, 3))
    (mixed,) = call(
        mixed_body, [((tokens, columns), BF16)], attended, other_attended, out_weight, other_rows, after=(four,)
    )
    grad_key, grad_value = call(
        down_z_body, [((tokens, columns), BF16)] * 2, near, four, back_5, back_7, back_1, back_3
    )
    (grad_weight,) = call(widen_body, [((columns, width), F32)], term, *others, vmem=6)
    return mixed, grad_query, grad_key, grad_value, grad_weight


def solution(mesh):
    finer = Mesh(mesh.devices.reshape(4, 4, 8, mesh.shape["head"]), (*SEQ, "head"))
    in_specs = (P(SEQ, "head"), P(SEQ, "head"), P(SEQ, "head"), P(SEQ, "head"), P("head", None))
    return jax.shard_map(
        per_device, mesh=finer, in_specs=in_specs, out_specs=in_specs, check_vma=False
    )
```

```python
import jax
import jax.numpy as jnp
from jax import lax
from jax.experimental import pallas as pl
from jax.experimental.pallas import tpu as pltpu
from jax.sharding import Mesh
from jax.sharding import PartitionSpec as P

HEAD_DIM = 64
POOL = 128
X, Y, Z = "seq_0", "seq_1", "seq_2"
SEQ = (X, Y, Z)
MIB = 1 << 20
F32 = jnp.float32
BF16 = jnp.bfloat16


def from_partner(value, axis, mask):
    pairs = [(source, source ^ mask) for source in range(lax.axis_size(axis))]
    return lax.ppermute(value, axis, pairs)


def to_others(values, axis, masks):
    return [from_partner(value, axis, mask) for value, mask in zip(values, masks)]


def call(body, outs, *args, scratch=(), vmem=4, after=(), through=(), flops=0):
    count, passed = len(args), len(after) + len(through)

    def ordered(*refs):
        made = refs[count + passed :]
        body(*refs[:count], *made[: len(outs)], *made[len(outs) + len(through) :])

    whole, anywhere = pl.BlockSpec(memory_space=pltpu.VMEM), pl.BlockSpec(memory_space=pl.ANY)
    return pl.pallas_call(
        ordered,
        out_shape=tuple(jax.ShapeDtypeStruct(shape, kind) for shape, kind in outs)
        + tuple(jax.ShapeDtypeStruct(value.shape, value.dtype) for value in through),
        in_specs=[whole] * count + [anywhere] * passed,
        out_specs=(whole,) * len(outs) + (anywhere,) * len(through),
        scratch_shapes=list(scratch),
        input_output_aliases={count + len(after) + at: len(outs) + at for at in range(len(through))},
        compiler_params=pltpu.CompilerParams(vmem_limit_bytes=vmem * MIB),
        cost_estimate=pl.CostEstimate(flops=flops, bytes_accessed=0, transcendentals=0) if flops else None,
    )(*args, *after, *through)


def iotas(rows, columns):
    return (
        lax.broadcasted_iota(jnp.int32, (rows, columns), 0),
        lax.broadcasted_iota(jnp.int32, (rows, columns), 1),
    )


def halved(values):
    rows = values.shape[0] // 2
    row, column = iotas(rows, 2 * rows)
    means = jnp.where((column >> 1) == row, 0.5, 0.0).astype(BF16)
    return jnp.dot(means, values, preferred_element_type=F32).astype(BF16)


def spread(values, height):
    values = values.astype(BF16)
    rows = values.shape[0] << height
    row, column = iotas(rows, values.shape[0])
    shares = jnp.where((row >> height) == column, 2.0**-height, 0.0).astype(BF16)
    return jnp.dot(shares, values, preferred_element_type=F32)


def wide(ref, start=0, rows=None):
    rows = ref.shape[0] - start if rows is None else rows
    return ref[start : start + rows].astype(F32)


def cut_at(side, columns):
    return pl.ds(pl.multiple_of(side * columns, columns), columns)


def pool_body(key_ref, value_ref, one_ref, two_ref, three_ref):
    columns = key_ref.shape[1]
    for at, ref in ((0, key_ref), (columns, value_ref)):
        one = halved(ref[...])
        two = halved(one)
        one_ref[:, at : at + columns] = one
        two_ref[:, at : at + columns] = two
        three_ref[:, at : at + columns] = halved(two)


def pair_body(three, from_1, pair_ref):
    pair_ref[:32] = three[...]
    pair_ref[32:] = halved(halved(from_1[...]))


def climb_z_body(pair, from_2, from_3, from_5, from_7, four_ref, five_ref):
    rows = [pair[...], halved(from_2[...]), halved(from_3[...]), from_5[...], from_7[...]]
    four = halved(jnp.concatenate(rows, axis=0))
    four_ref[...] = four
    five_ref[...] = halved(four)


def climb_y_body(five, from_1, from_2, from_3, six_ref, seven_ref):
    rows = [five[...], halved(from_1[...]), from_2[...], from_3[...]]
    six = halved(jnp.concatenate(rows, axis=0))
    six_ref[...] = six
    seven_ref[...] = halved(six)


PAIR = 2 * HEAD_DIM
NT = (((1,), (1,)), ((), ()))
TN = (((0,), (0,)), ((), ()))


def first_head(rows):
    return lax.broadcasted_iota(jnp.int32, (rows, PAIR), 1) < HEAD_DIM


def by_head(block):
    first, zero = first_head(block.shape[0]), jnp.zeros_like(block)
    return jnp.concatenate([jnp.where(first, block, zero), jnp.where(first, zero, block)], axis=0)


def side_by_side(block):
    rows = block.shape[0] // 2
    return jnp.where(first_head(rows), block[:rows], block[rows:])


def scaled(block):
    return block * jnp.asarray(HEAD_DIM**-0.5, BF16)


def forward_body(*refs):
    query, key, value = refs[:3]
    pieces = refs[3:14]
    attended_ref, probs_ref, listed = refs[14:17]
    quarter_refs = refs[17:21]
    tokens, columns = query.shape
    listed[:tokens, :columns] = key[...]
    listed[:tokens, columns:] = value[...]
    at = tokens
    for piece in pieces:
        rows = piece.shape[0]
        listed[at : at + rows] = piece[...]
        at += rows
    for pair in range(columns // PAIR):
        cut = slice(pair * PAIR, (pair + 1) * PAIR)
        cut_v = slice(columns + pair * PAIR, columns + (pair + 1) * PAIR)
        queries = by_head(scaled(query[:, cut]))
        scores = lax.dot_general(queries, listed[:, cut], NT, preferred_element_type=F32)
        powers = jnp.exp(scores - jnp.max(scores, axis=1, keepdims=True))
        probs = powers * (1.0 / jnp.sum(powers, axis=1, keepdims=True))
        probs_ref[pair] = probs
        attended_ref[:, cut] = side_by_side(
            jnp.dot(probs.astype(BF16), listed[:, cut_v], preferred_element_type=F32)
        ).astype(BF16)
    me = lax.axis_index(Y)
    for mask, ref in enumerate(quarter_refs):
        ref[...] = attended_ref[:, cut_at(me ^ mask, POOL)]


def backward_body(*refs):
    query, grad, listed, probs_ref = refs[:4]
    grad_query_ref, near_ref = refs[4:6]
    far_refs = refs[6:]
    tokens, columns = query.shape
    for pair in range(columns // PAIR):
        cut = slice(pair * PAIR, (pair + 1) * PAIR)
        cut_v = slice(columns + pair * PAIR, columns + (pair + 1) * PAIR)
        keys, values = listed[:, cut], listed[:, cut_v]
        queries = by_head(scaled(query[:, cut]))
        grads = by_head(grad[:, cut])
        probs = probs_ref[pair]
        weights = probs.astype(BF16)
        grad_probs = lax.dot_general(grads, values, NT, preferred_element_type=F32)
        centred = jnp.sum(probs * grad_probs, axis=1, keepdims=True)
        grad_scores = (probs * (grad_probs - centred)).astype(BF16)
        grad_query_ref[:, cut] = (
            side_by_side(jnp.dot(grad_scores, keys, preferred_element_type=F32)) * HEAD_DIM**-0.5
        ).astype(BF16)
        for where, left, right in ((cut, grad_scores, queries), (cut_v, weights, grads)):
            total = lax.dot_general(left, right, TN, preferred_element_type=F32)
            near_ref[:, where] = total[:tokens]
            at = tokens
            for ref in far_refs:
                rows = ref.shape[0]
                ref[:, where] = total[at : at + rows].astype(BF16)
                at += rows


def down_x_body(mine, own_term, back_1, back_2, back_3, carry_ref, one_ref, two_ref, three_ref, term_ref):
    six = wide(back_1, 0, 128) + spread(wide(back_2, 0, 64) + wide(back_3, 0, 64), 1)
    carry_ref[...] = spread(six[:32], 2).astype(BF16)
    one_ref[...] = (wide(mine, 0, 128) + spread(six[32:64], 2)).astype(BF16)
    two_ref[...] = (wide(mine, 128, 64) + spread(six[64:96], 1)).astype(BF16)
    three_ref[...] = (wide(mine, 192, 64) + spread(six[96:], 1)).astype(BF16)
    term = wide(own_term) + wide(back_1, 128, 32) + wide(back_2, 64, 32) + wide(back_3, 64, 32)
    term_ref[...] = term.astype(BF16)


def down_y_body(mine, carry, back_1, back_2, back_3, four_ref, two_ref, three_ref, five_ref, seven_ref):
    four = wide(carry) + wide(back_1) + spread(wide(back_2) + wide(back_3), 1)
    four_ref[...] = four.astype(BF16)
    two_ref[...] = (wide(mine, 128, 64) + spread(four[32:48], 2)).astype(BF16)
    three_ref[...] = (wide(mine, 192, 64) + spread(four[48:64], 2)).astype(BF16)
    five_ref[...] = (wide(mine, 256, 64) + spread(four[64:96], 1)).astype(BF16)
    seven_ref[...] = (wide(mine, 320, 64) + spread(four[96:], 1)).astype(BF16)


def down_pair_body(mine, four, back_5, back_7, one_ref):
    total = wide(mine, 0, 128) + spread(wide(four, 16, 16), 3)
    total = total + spread(wide(back_5, 32, 32) + wide(back_7, 32, 32), 2)
    one_ref[...] = total.astype(BF16)


def down_z_body(near, four, back_1, back_2, back_3, back_5, back_7, key_ref, value_ref):
    columns = key_ref.shape[1]
    total = near[...] + spread(wide(four, 0, 16), 4) + spread(back_1[...], 1)
    total = total + spread(wide(back_2) + wide(back_3), 2)
    total = total + spread(wide(back_5, 0, 32) + wide(back_7, 0, 32), 3)
    key_ref[...] = total[:, :columns].astype(BF16)
    value_ref[...] = total[:, columns:].astype(BF16)


def weight_body(*refs):
    lefts, own_grads, other_grads, far_refs = refs[:4], refs[4:8], refs[8:12], refs[12:15]
    out_refs, total_ref = refs[15:19], refs[19]
    columns = own_grads[0].shape[1]
    me, head = lax.axis_index(X), lax.axis_index("head")
    for side, rights in ((head, own_grads), (1 - head, other_grads)):
        total = None
        for left, right in zip(lefts, rights):
            part = lax.dot_general(left[...], right[...], TN, preferred_element_type=F32)
            total = part if total is None else total + part
        total_ref[:, cut_at(side, columns)] = total * (1.0 / 32768)
    for mask, ref in enumerate(out_refs):
        rows = ref.shape[0] - 32
        if mask:
            ref[:rows] = far_refs[mask - 1][...]
        ref[rows:] = total_ref[pl.ds(pl.multiple_of((me ^ mask) * 32, 32), 32)].astype(BF16)


def sum_body(*refs):
    total = wide(refs[0])
    for ref in refs[1:-1]:
        total = total + wide(ref)
    refs[-1][...] = total.astype(BF16)


def join_body(*refs):
    me = lax.axis_index(X)
    out_ref = refs[4]
    for mask, ref in enumerate(refs[:4]):
        out_ref[pl.ds(pl.multiple_of((me ^ mask) * 32, 32), 32)] = ref[...]


def widen_body(*refs):
    me = lax.axis_index(Y)
    out_ref = refs[4]
    for mask, ref in enumerate(refs[:4]):
        out_ref[cut_at(me ^ mask, POOL)] = wide(ref)


def columns_body(weight, out_ref):
    columns = out_ref.shape[1]
    out_ref[...] = weight[:, cut_at(1 - lax.axis_index("head"), columns)]


def grad_in_body(own, other, weight, out_ref):
    columns = own.shape[1]
    head = lax.axis_index("head")
    nt = (((1,), (1,)), ((), ()))
    total = lax.dot_general(own[...], weight[:, cut_at(head, columns)], nt, preferred_element_type=F32)
    total = total + lax.dot_general(
        other[...], weight[:, cut_at(1 - head, columns)], nt, preferred_element_type=F32
    )
    out_ref[...] = total.astype(BF16)


def mixed_body(own, other, weight, other_rows, out_ref):
    columns = own.shape[1]
    own_rows = weight[:, cut_at(lax.axis_index("head"), columns)]
    total = jnp.dot(own[...], own_rows, preferred_element_type=F32)
    total = total + jnp.dot(other[...], other_rows[...], preferred_element_type=F32)
    out_ref[...] = total.astype(BF16)


def per_device(query, key, value, grad_out, out_weight):
    tokens, columns = query.shape
    width = 2 * columns

    def rows(*counts):
        return [((count, width), BF16) for count in counts]

    one, two, three = call(pool_body, rows(128, 64, 32), key, value)
    z_1, z_2, z_3 = to_others((one, two, two), Z, (1, 2, 3))
    grads = [grad_out] + to_others([grad_out] * 3, Y, (1, 2, 3))
    (pair,) = call(pair_body, rows(64), three, z_1)
    z_5, z_7 = to_others((pair, pair), Z, (5, 7))
    four, five = call(climb_z_body, rows(128, 64), pair, z_2, z_3, z_5, z_7, after=grads[1:])
    y_1, y_2, y_3 = to_others((four, five, five), Y, (1, 2, 3))
    other_grads = [from_partner(grad, "head", 1) for grad in grads]
    (other_rows,) = call(columns_body, [((columns, columns), BF16)], out_weight)
    other_rows = from_partner(other_rows, "head", 1)
    (grad_in,) = call(grad_in_body, [((tokens, columns), BF16)], grad_out, other_grads[0], out_weight)
    six, seven = call(climb_y_body, rows(128, 64), five, y_1, y_2, y_3)
    x_1, x_2, x_3 = to_others((six, seven, seven), X, (1, 2, 3))
    listed_rows = tokens + 7 * POOL
    attended, probs, listed, *quarters = call(
        forward_body,
        [((tokens, columns), BF16), ((columns // PAIR, 2 * tokens, listed_rows), F32), ((listed_rows, width), BF16)]
        + [((tokens, POOL), BF16)] * 4,
        query, key, value, x_1, x_2, x_3, y_1, y_2, y_3, z_1, z_2, z_3, z_5, z_7,
        vmem=12,
        flops=6 * 10**9,
        after=(other_rows, *other_grads),
    )
    quarters = [quarters[0]] + to_others(quarters[1:], Y, (1, 2, 3))
    grad_query, near, far_x_1, far_x_2, far_x_3, far_y, far_z = call(
        backward_body,
        [((tokens, columns), BF16), ((tokens, width), F32)] + rows(128, 64, 64, 256, 384),
        query, grad_in, listed, probs,
        vmem=16,
        flops=8 * 10**9,
    )
    own_term, *to_x = call(
        weight_body, rows(32, 160, 96, 96), *quarters, *grads, *other_grads, far_x_1, far_x_2, far_x_3,
        scratch=[pltpu.VMEM((POOL, width), F32)],
    )
    back_x = to_others(to_x, X, (1, 2, 3))
    carry, *to_y, term = call(down_x_body, rows(128, 128, 64, 64, 32), far_y, own_term, *back_x)
    back_y = to_others(to_y, Y, (1, 2, 3))
    other_attended = from_partner(attended, "head", 1)
    for mask in (1, 3, 7):
        (term,) = call(sum_body, rows(32), term, from_partner(term, Z, mask))
    four, *to_z = call(down_y_body, rows(128, 64, 64, 64, 64), far_z, carry, *back_y)
    back_2, back_3, back_5, back_7 = to_others(to_z, Z, (2, 3, 5, 7))
    (term,) = call(join_body, rows(128), term, *to_others([term] * 3, X, (1, 2, 3)))
    (to_1,) = call(down_pair_body, rows(128), far_z, four, back_5, back_7, after=(back_3,))
    back_1 = from_partner(to_1, Z, 1)
    others = to_others([term] * 3, Y, (1, 2, 3))
    (mixed,) = call(
        mixed_body, [((tokens, columns), BF16)], attended, other_attended, out_weight, other_rows, after=(four,)
    )
    grad_key, grad_value = call(
        down_z_body, [((tokens, columns), BF16)] * 2, near, four, back_1, back_2, back_3, back_5, back_7
    )
    (grad_weight,) = call(widen_body, [((columns, width), F32)], term, *others, vmem=6)
    return mixed, grad_query, grad_key, grad_value, grad_weight


def solution(mesh):
    finer = Mesh(mesh.devices.reshape(4, 4, 8, mesh.shape["head"]), (*SEQ, "head"))
    in_specs = (P(SEQ, "head"), P(SEQ, "head"), P(SEQ, "head"), P(SEQ, "head"), P("head", None))
    return jax.shard_map(
        per_device, mesh=finer, in_specs=in_specs, out_specs=in_specs, check_vma=False
    )
```

```python
import jax
import jax.numpy as jnp
from jax import lax
from jax.experimental import pallas as pl
from jax.experimental.pallas import tpu as pltpu
from jax.sharding import Mesh
from jax.sharding import PartitionSpec as P

HEAD_DIM = 64
POOL = 128
X, Y, Z = "seq_0", "seq_1", "seq_2"
SEQ = (X, Y, Z)
MIB = 1 << 20
F32 = jnp.float32
BF16 = jnp.bfloat16


def from_partner(value, axis, mask):
    pairs = [(source, source ^ mask) for source in range(lax.axis_size(axis))]
    return lax.ppermute(value, axis, pairs)


def to_others(values, axis, masks):
    return [from_partner(value, axis, mask) for value, mask in zip(values, masks)]


def call(body, outs, *args, scratch=(), vmem=4, after=(), through=(), flops=0):
    count, passed = len(args), len(after) + len(through)

    def ordered(*refs):
        made = refs[count + passed :]
        body(*refs[:count], *made[: len(outs)], *made[len(outs) + len(through) :])

    whole, anywhere = pl.BlockSpec(memory_space=pltpu.VMEM), pl.BlockSpec(memory_space=pl.ANY)
    return pl.pallas_call(
        ordered,
        out_shape=tuple(jax.ShapeDtypeStruct(shape, kind) for shape, kind in outs)
        + tuple(jax.ShapeDtypeStruct(value.shape, value.dtype) for value in through),
        in_specs=[whole] * count + [anywhere] * passed,
        out_specs=(whole,) * len(outs) + (anywhere,) * len(through),
        scratch_shapes=list(scratch),
        input_output_aliases={count + len(after) + at: len(outs) + at for at in range(len(through))},
        compiler_params=pltpu.CompilerParams(vmem_limit_bytes=vmem * MIB),
        cost_estimate=pl.CostEstimate(flops=flops, bytes_accessed=0, transcendentals=0) if flops else None,
    )(*args, *after, *through)


def iotas(rows, columns):
    return (
        lax.broadcasted_iota(jnp.int32, (rows, columns), 0),
        lax.broadcasted_iota(jnp.int32, (rows, columns), 1),
    )


def halved(values):
    rows = values.shape[0] // 2
    row, column = iotas(rows, 2 * rows)
    means = jnp.where((column >> 1) == row, 0.5, 0.0).astype(BF16)
    return jnp.dot(means, values, preferred_element_type=F32).astype(BF16)


def spread(values, height):
    values = values.astype(BF16)
    rows = values.shape[0] << height
    row, column = iotas(rows, values.shape[0])
    shares = jnp.where((row >> height) == column, 2.0**-height, 0.0).astype(BF16)
    return jnp.dot(shares, values, preferred_element_type=F32)


def wide(ref, start=0, rows=None):
    rows = ref.shape[0] - start if rows is None else rows
    return ref[start : start + rows].astype(F32)


def cut_at(side, columns):
    return pl.ds(pl.multiple_of(side * columns, columns), columns)


def pool_body(key_ref, value_ref, one_ref, two_ref, three_ref):
    columns = key_ref.shape[1]
    for at, ref in ((0, key_ref), (columns, value_ref)):
        one = halved(ref[...])
        two = halved(one)
        one_ref[:, at : at + columns] = one
        two_ref[:, at : at + columns] = two
        three_ref[:, at : at + columns] = halved(two)


def pair_body(three, from_1, two_ref, pair_ref):
    two = halved(from_1[...])
    two_ref[...] = two
    pair_ref[:32] = three[...]
    pair_ref[32:] = halved(two)


def climb_z_body(pair, from_3, beside_3, from_5, from_7, four_ref, five_ref):
    rows = [pair[...], halved(from_3[...]), halved(beside_3[...]), from_5[...], from_7[...]]
    four = halved(jnp.concatenate(rows, axis=0))
    four_ref[...] = four
    five_ref[...] = halved(four)


def climb_y_body(five, from_1, from_2, from_3, six_ref, seven_ref):
    rows = [five[...], halved(from_1[...]), from_2[...], from_3[...]]
    six = halved(jnp.concatenate(rows, axis=0))
    six_ref[...] = six
    seven_ref[...] = halved(six)


PAIR = 2 * HEAD_DIM
NT = (((1,), (1,)), ((), ()))
TN = (((0,), (0,)), ((), ()))


def first_head(rows):
    return lax.broadcasted_iota(jnp.int32, (rows, PAIR), 1) < HEAD_DIM


def by_head(block):
    first, zero = first_head(block.shape[0]), jnp.zeros_like(block)
    return jnp.concatenate([jnp.where(first, block, zero), jnp.where(first, zero, block)], axis=0)


def side_by_side(block):
    rows = block.shape[0] // 2
    return jnp.where(first_head(rows), block[:rows], block[rows:])


def scaled(block):
    return block * jnp.asarray(HEAD_DIM**-0.5, BF16)


def forward_body(*refs):
    query, key, value = refs[:3]
    pieces = refs[3:14]
    attended_ref, probs_ref, listed = refs[14:17]
    quarter_refs = refs[17:21]
    tokens, columns = query.shape
    listed[:tokens, :columns] = key[...]
    listed[:tokens, columns:] = value[...]
    at = tokens
    for piece in pieces:
        rows = piece.shape[0]
        listed[at : at + rows] = piece[...]
        at += rows
    for pair in range(columns // PAIR):
        cut = slice(pair * PAIR, (pair + 1) * PAIR)
        cut_v = slice(columns + pair * PAIR, columns + (pair + 1) * PAIR)
        queries = by_head(scaled(query[:, cut]))
        scores = lax.dot_general(queries, listed[:, cut], NT, preferred_element_type=F32)
        powers = jnp.exp(scores - jnp.max(scores, axis=1, keepdims=True))
        probs = powers * (1.0 / jnp.sum(powers, axis=1, keepdims=True))
        probs_ref[pair] = probs
        attended_ref[:, cut] = side_by_side(
            jnp.dot(probs.astype(BF16), listed[:, cut_v], preferred_element_type=F32)
        ).astype(BF16)
    me = lax.axis_index(X)
    for mask, ref in enumerate(quarter_refs):
        ref[...] = attended_ref[:, cut_at(me ^ mask, POOL)]


def backward_body(*refs):
    query, grad, listed, probs_ref = refs[:4]
    grad_query_ref, near_ref = refs[4:6]
    far_refs = refs[6:]
    tokens, columns = query.shape
    for pair in range(columns // PAIR):
        cut = slice(pair * PAIR, (pair + 1) * PAIR)
        cut_v = slice(columns + pair * PAIR, columns + (pair + 1) * PAIR)
        keys, values = listed[:, cut], listed[:, cut_v]
        queries = by_head(scaled(query[:, cut]))
        grads = by_head(grad[:, cut])
        probs = probs_ref[pair]
        weights = probs.astype(BF16)
        grad_probs = lax.dot_general(grads, values, NT, preferred_element_type=F32)
        centred = jnp.sum(probs * grad_probs, axis=1, keepdims=True)
        grad_scores = (probs * (grad_probs - centred)).astype(BF16)
        grad_query_ref[:, cut] = (
            side_by_side(jnp.dot(grad_scores, keys, preferred_element_type=F32)) * HEAD_DIM**-0.5
        ).astype(BF16)
        for where, left, right in ((cut, grad_scores, queries), (cut_v, weights, grads)):
            total = lax.dot_general(left, right, TN, preferred_element_type=F32)
            near_ref[:, where] = total[:tokens]
            at = tokens
            for ref in far_refs:
                rows = ref.shape[0]
                ref[:, where] = total[at : at + rows].astype(BF16)
                at += rows


def down_x_body(mine, back_1, back_2, back_3, carry_ref, one_ref, two_ref, three_ref):
    six = wide(back_1) + spread(wide(back_2) + wide(back_3), 1)
    carry_ref[...] = spread(six[:32], 2).astype(BF16)
    one_ref[...] = (wide(mine, 0, 128) + spread(six[32:64], 2)).astype(BF16)
    two_ref[...] = (wide(mine, 128, 64) + spread(six[64:96], 1)).astype(BF16)
    three_ref[...] = (wide(mine, 192, 64) + spread(six[96:], 1)).astype(BF16)


def down_y_body(mine, carry, back_1, back_2, back_3, four_ref, beside_ref, five_ref, seven_ref):
    four = wide(carry) + wide(back_1) + spread(wide(back_2) + wide(back_3), 1)
    four_ref[...] = four.astype(BF16)
    beside_ref[...] = (wide(mine, 192, 64) + spread(four[48:64], 2)).astype(BF16)
    five_ref[...] = (wide(mine, 256, 64) + spread(four[64:96], 1)).astype(BF16)
    seven_ref[...] = (wide(mine, 320, 64) + spread(four[96:], 1)).astype(BF16)


def down_pair_body(mine, four, beside, back_5, back_7, one_ref, three_ref):
    total = wide(mine, 0, 128) + spread(wide(four, 16, 16), 3) + spread(beside[...], 1)
    total = total + spread(wide(back_5, 32, 32) + wide(back_7, 32, 32), 2)
    one_ref[...] = total.astype(BF16)
    three_ref[...] = (wide(mine, 128, 64) + spread(wide(four, 32, 16), 2)).astype(BF16)


def down_z_body(near, four, back_5, back_7, back_1, back_3, key_ref, value_ref):
    columns = key_ref.shape[1]
    total = near[...] + spread(wide(four, 0, 16), 4) + spread(back_1[...], 1) + spread(back_3[...], 2)
    total = total + spread(wide(back_5, 0, 32) + wide(back_7, 0, 32), 3)
    key_ref[...] = total[:, :columns].astype(BF16)
    value_ref[...] = total[:, columns:].astype(BF16)


def weight_body(*refs):
    lefts, own_grads, other_grads, out_refs, total_ref = refs[:4], refs[4:8], refs[8:12], refs[12:16], refs[16]
    columns = own_grads[0].shape[1]
    me, head = lax.axis_index(Y), lax.axis_index("head")
    for side, rights in ((head, own_grads), (1 - head, other_grads)):
        total = None
        for left, right in zip(lefts, rights):
            part = lax.dot_general(left[...], right[...], TN, preferred_element_type=F32)
            total = part if total is None else total + part
        total_ref[:, cut_at(side, columns)] = total * (1.0 / 32768)
    for mask, ref in enumerate(out_refs):
        ref[...] = total_ref[pl.ds(pl.multiple_of((me ^ mask) * 32, 32), 32)].astype(BF16)


def sum_body(*refs):
    total = wide(refs[0])
    for ref in refs[1:-1]:
        total = total + wide(ref)
    refs[-1][...] = total.astype(BF16)


def join_body(*refs):
    me = lax.axis_index(Y)
    out_ref = refs[4]
    for mask, ref in enumerate(refs[:4]):
        out_ref[pl.ds(pl.multiple_of((me ^ mask) * 32, 32), 32)] = ref[...]


def widen_body(*refs):
    me = lax.axis_index(X)
    out_ref = refs[4]
    for mask, ref in enumerate(refs[:4]):
        out_ref[cut_at(me ^ mask, POOL)] = wide(ref)


def columns_body(weight, out_ref):
    columns = out_ref.shape[1]
    out_ref[...] = weight[:, cut_at(1 - lax.axis_index("head"), columns)]


def grad_in_body(own, other, weight, out_ref):
    columns = own.shape[1]
    head = lax.axis_index("head")
    nt = (((1,), (1,)), ((), ()))
    total = lax.dot_general(own[...], weight[:, cut_at(head, columns)], nt, preferred_element_type=F32)
    total = total + lax.dot_general(
        other[...], weight[:, cut_at(1 - head, columns)], nt, preferred_element_type=F32
    )
    out_ref[...] = total.astype(BF16)


def mixed_body(own, other, weight, other_rows, out_ref):
    columns = own.shape[1]
    own_rows = weight[:, cut_at(lax.axis_index("head"), columns)]
    total = jnp.dot(own[...], own_rows, preferred_element_type=F32)
    total = total + jnp.dot(other[...], other_rows[...], preferred_element_type=F32)
    out_ref[...] = total.astype(BF16)


def per_device(query, key, value, grad_out, out_weight):
    tokens, columns = query.shape
    width = 2 * columns

    def rows(*counts):
        return [((count, width), BF16) for count in counts]

    one, two, three = call(pool_body, rows(128, 64, 32), key, value)
    z_1 = from_partner(one, Z, 1)
    z_3 = from_partner(two, Z, 3)
    grads = [grad_out] + to_others([grad_out] * 3, X, (1, 2, 3))
    two, pair = call(pair_body, rows(64, 64), three, z_1)
    beside_3, z_5, z_7 = to_others((two, pair, pair), Z, (3, 5, 7))
    four, five = call(climb_z_body, rows(128, 64), pair, z_3, beside_3, z_5, z_7, after=grads[1:])
    y_1, y_2, y_3 = to_others((four, five, five), Y, (1, 2, 3))
    other_grads = [from_partner(grad, "head", 1) for grad in grads]
    (other_rows,) = call(columns_body, [((columns, columns), BF16)], out_weight)
    other_rows = from_partner(other_rows, "head", 1)
    (grad_in,) = call(grad_in_body, [((tokens, columns), BF16)], grad_out, other_grads[0], out_weight)
    six, seven = call(climb_y_body, rows(128, 64), five, y_1, y_2, y_3)
    x_1, x_2, x_3 = to_others((six, seven, seven), X, (1, 2, 3))
    listed_rows = tokens + 7 * POOL
    attended, probs, listed, *quarters = call(
        forward_body,
        [((tokens, columns), BF16), ((columns // PAIR, 2 * tokens, listed_rows), F32), ((listed_rows, width), BF16)]
        + [((tokens, POOL), BF16)] * 4,
        query, key, value, x_1, x_2, x_3, y_1, y_2, y_3, z_1, z_3, beside_3, z_5, z_7,
        vmem=12,
        flops=6 * 10**9,
        after=(other_rows, *other_grads),
    )
    quarters = [quarters[0]] + to_others(quarters[1:], X, (1, 2, 3))
    grad_query, near, far_x_1, far_x_2, far_x_3, far_y, far_z = call(
        backward_body,
        [((tokens, columns), BF16), ((tokens, width), F32)] + rows(128, 64, 64, 256, 384),
        query, grad_in, listed, probs,
        vmem=16,
        flops=8 * 10**9,
    )
    *terms, far_x_1, far_x_2, far_x_3 = call(
        weight_body, rows(32, 32, 32, 32), *quarters, *grads, *other_grads,
        scratch=[pltpu.VMEM((POOL, width), F32)],
        through=(far_x_1, far_x_2, far_x_3),
    )
    back_x = to_others((far_x_1, far_x_2, far_x_3), X, (1, 2, 3))
    terms = [terms[0]] + to_others(terms[1:], Y, (1, 2, 3))
    carry, *to_y = call(down_x_body, rows(128, 128, 64, 64), far_y, *back_x, after=terms[1:])
    back_y = to_others(to_y, Y, (1, 2, 3))
    other_attended = from_partner(attended, "head", 1)
    (term,) = call(sum_body, rows(32), *terms)
    others = to_others([term] * 3, Z, (3, 5, 6))
    four, beside, to_5, to_7 = call(
        down_y_body, rows(128, 64, 64, 64), far_z, carry, *back_y, after=others
    )
    beside, back_5, back_7 = to_others((beside, to_5, to_7), Z, (3, 5, 7))
    (term,) = call(sum_body, rows(32), term, *others, after=(four,))
    (term,) = call(sum_body, rows(32), term, from_partner(term, Z, 1))
    (term,) = call(join_body, rows(128), term, *to_others([term] * 3, Y, (1, 2, 3)))
    to_1, to_3 = call(down_pair_body, rows(128, 64), far_z, four, beside, back_5, back_7, after=(term,))
    back_1, back_3 = to_others((to_1, to_3), Z, (1, 3))
    others = to_others([term] * 3, X, (1, 2, 3))
    (mixed,) = call(
        mixed_body, [((tokens, columns), BF16)], attended, other_attended, out_weight, other_rows, after=(four,)
    )
    grad_key, grad_value = call(
        down_z_body, [((tokens, columns), BF16)] * 2, near, four, back_5, back_7, back_1, back_3
    )
    (grad_weight,) = call(widen_body, [((columns, width), F32)], term, *others, vmem=6)
    return mixed, grad_query, grad_key, grad_value, grad_weight


def solution(mesh):
    finer = Mesh(mesh.devices.reshape(4, 4, 8, mesh.shape["head"]), (*SEQ, "head"))
    in_specs = (P(SEQ, "head"), P(SEQ, "head"), P(SEQ, "head"), P(SEQ, "head"), P("head", None))
    return jax.shard_map(
        per_device, mesh=finer, in_specs=in_specs, out_specs=in_specs, check_vma=False
    )
```

```python
import jax
import jax.numpy as jnp
from jax import lax
from jax.experimental import pallas as pl
from jax.experimental.pallas import tpu as pltpu
from jax.sharding import Mesh
from jax.sharding import PartitionSpec as P

HEAD_DIM = 64
POOL = 128
X, Y, Z = "seq_0", "seq_1", "seq_2"
SEQ = (X, Y, Z)
MIB = 1 << 20
F32 = jnp.float32
BF16 = jnp.bfloat16


def from_partner(value, axis, mask):
    pairs = [(source, source ^ mask) for source in range(lax.axis_size(axis))]
    return lax.ppermute(value, axis, pairs)


def to_others(values, axis, masks):
    return [from_partner(value, axis, mask) for value, mask in zip(values, masks)]


def call(body, outs, *args, scratch=(), vmem=4, after=(), through=(), flops=0):
    count, passed = len(args), len(after) + len(through)

    def ordered(*refs):
        made = refs[count + passed :]
        body(*refs[:count], *made[: len(outs)], *made[len(outs) + len(through) :])

    whole, anywhere = pl.BlockSpec(memory_space=pltpu.VMEM), pl.BlockSpec(memory_space=pl.ANY)
    return pl.pallas_call(
        ordered,
        out_shape=tuple(jax.ShapeDtypeStruct(shape, kind) for shape, kind in outs)
        + tuple(jax.ShapeDtypeStruct(value.shape, value.dtype) for value in through),
        in_specs=[whole] * count + [anywhere] * passed,
        out_specs=(whole,) * len(outs) + (anywhere,) * len(through),
        scratch_shapes=list(scratch),
        input_output_aliases={count + len(after) + at: len(outs) + at for at in range(len(through))},
        compiler_params=pltpu.CompilerParams(vmem_limit_bytes=vmem * MIB),
        cost_estimate=pl.CostEstimate(flops=flops, bytes_accessed=0, transcendentals=0) if flops else None,
    )(*args, *after, *through)


def iotas(rows, columns):
    return (
        lax.broadcasted_iota(jnp.int32, (rows, columns), 0),
        lax.broadcasted_iota(jnp.int32, (rows, columns), 1),
    )


def halved(values):
    rows = values.shape[0] // 2
    row, column = iotas(rows, 2 * rows)
    means = jnp.where((column >> 1) == row, 0.5, 0.0).astype(BF16)
    return jnp.dot(means, values, preferred_element_type=F32).astype(BF16)


def spread(values, height):
    values = values.astype(BF16)
    rows = values.shape[0] << height
    row, column = iotas(rows, values.shape[0])
    shares = jnp.where((row >> height) == column, 2.0**-height, 0.0).astype(BF16)
    return jnp.dot(shares, values, preferred_element_type=F32)


def wide(ref, start=0, rows=None):
    rows = ref.shape[0] - start if rows is None else rows
    return ref[start : start + rows].astype(F32)


def cut_at(side, columns):
    return pl.ds(pl.multiple_of(side * columns, columns), columns)


def pool_body(key_ref, value_ref, one_ref, two_ref, three_ref):
    columns = key_ref.shape[1]
    for at, ref in ((0, key_ref), (columns, value_ref)):
        one = halved(ref[...])
        two = halved(one)
        one_ref[:, at : at + columns] = one
        two_ref[:, at : at + columns] = two
        three_ref[:, at : at + columns] = halved(two)


def pair_body(three, from_1, two_ref, pair_ref):
    two = halved(from_1[...])
    two_ref[...] = two
    pair_ref[:32] = three[...]
    pair_ref[32:] = halved(two)


def climb_z_body(pair, from_3, beside_3, from_5, from_7, four_ref, five_ref):
    rows = [pair[...], halved(from_3[...]), halved(beside_3[...]), from_5[...], from_7[...]]
    four = halved(jnp.concatenate(rows, axis=0))
    four_ref[...] = four
    five_ref[...] = halved(four)


def climb_y_body(five, from_1, from_2, from_3, six_ref, seven_ref):
    rows = [five[...], halved(from_1[...]), from_2[...], from_3[...]]
    six = halved(jnp.concatenate(rows, axis=0))
    six_ref[...] = six
    seven_ref[...] = halved(six)


PAIR = 2 * HEAD_DIM
NT = (((1,), (1,)), ((), ()))
TN = (((0,), (0,)), ((), ()))


def first_head(rows):
    return lax.broadcasted_iota(jnp.int32, (rows, PAIR), 1) < HEAD_DIM


def by_head(block):
    first, zero = first_head(block.shape[0]), jnp.zeros_like(block)
    return jnp.concatenate([jnp.where(first, block, zero), jnp.where(first, zero, block)], axis=0)


def side_by_side(block):
    rows = block.shape[0] // 2
    return jnp.where(first_head(rows), block[:rows], block[rows:])


def scaled(block):
    return block * jnp.asarray(HEAD_DIM**-0.5, BF16)


def forward_body(*refs):
    query, key, value = refs[:3]
    pieces = refs[3:14]
    attended_ref, probs_ref, listed = refs[14:17]
    quarter_refs = refs[17:21]
    tokens, columns = query.shape
    listed[:tokens, :columns] = key[...]
    listed[:tokens, columns:] = value[...]
    at = tokens
    for piece in pieces:
        rows = piece.shape[0]
        listed[at : at + rows] = piece[...]
        at += rows
    for pair in range(columns // PAIR):
        cut = slice(pair * PAIR, (pair + 1) * PAIR)
        cut_v = slice(columns + pair * PAIR, columns + (pair + 1) * PAIR)
        queries = by_head(scaled(query[:, cut]))
        scores = lax.dot_general(queries, listed[:, cut], NT, preferred_element_type=F32)
        powers = jnp.exp(scores - jnp.max(scores, axis=1, keepdims=True))
        probs = powers * (1.0 / jnp.sum(powers, axis=1, keepdims=True))
        probs_ref[pair] = probs
        attended_ref[:, cut] = side_by_side(
            jnp.dot(probs.astype(BF16), listed[:, cut_v], preferred_element_type=F32)
        ).astype(BF16)
    me = lax.axis_index(X)
    for mask, ref in enumerate(quarter_refs):
        ref[...] = attended_ref[:, cut_at(me ^ mask, POOL)]


def backward_body(*refs):
    query, grad, listed, probs_ref = refs[:4]
    grad_query_ref, near_ref = refs[4:6]
    far_refs = refs[6:]
    tokens, columns = query.shape
    for pair in range(columns // PAIR):
        cut = slice(pair * PAIR, (pair + 1) * PAIR)
        cut_v = slice(columns + pair * PAIR, columns + (pair + 1) * PAIR)
        keys, values = listed[:, cut], listed[:, cut_v]
        queries = by_head(scaled(query[:, cut]))
        grads = by_head(grad[:, cut])
        probs = probs_ref[pair]
        weights = probs.astype(BF16)
        grad_probs = lax.dot_general(grads, values, NT, preferred_element_type=F32)
        centred = jnp.sum(probs * grad_probs, axis=1, keepdims=True)
        grad_scores = (probs * (grad_probs - centred)).astype(BF16)
        grad_query_ref[:, cut] = (
            side_by_side(jnp.dot(grad_scores, keys, preferred_element_type=F32)) * HEAD_DIM**-0.5
        ).astype(BF16)
        for where, left, right in ((cut, grad_scores, queries), (cut_v, weights, grads)):
            total = lax.dot_general(left, right, TN, preferred_element_type=F32)
            near_ref[:, where] = total[:tokens]
            at = tokens
            for ref in far_refs:
                rows = ref.shape[0]
                ref[:, where] = total[at : at + rows].astype(BF16)
                at += rows


def down_x_body(mine, back_1, back_2, back_3, carry_ref, one_ref, two_ref, three_ref):
    six = wide(back_1) + spread(wide(back_2) + wide(back_3), 1)
    carry_ref[...] = spread(six[:32], 2).astype(BF16)
    one_ref[...] = (wide(mine, 0, 128) + spread(six[32:64], 2)).astype(BF16)
    two_ref[...] = (wide(mine, 128, 64) + spread(six[64:96], 1)).astype(BF16)
    three_ref[...] = (wide(mine, 192, 64) + spread(six[96:], 1)).astype(BF16)


def down_y_body(mine, carry, back_1, back_2, back_3, four_ref, beside_ref, five_ref, seven_ref):
    four = wide(carry) + wide(back_1) + spread(wide(back_2) + wide(back_3), 1)
    four_ref[...] = four.astype(BF16)
    beside_ref[...] = (wide(mine, 192, 64) + spread(four[48:64], 2)).astype(BF16)
    five_ref[...] = (wide(mine, 256, 64) + spread(four[64:96], 1)).astype(BF16)
    seven_ref[...] = (wide(mine, 320, 64) + spread(four[96:], 1)).astype(BF16)


def down_pair_body(mine, four, beside, back_5, back_7, one_ref, three_ref):
    total = wide(mine, 0, 128) + spread(wide(four, 16, 16), 3) + spread(beside[...], 1)
    total = total + spread(wide(back_5, 32, 32) + wide(back_7, 32, 32), 2)
    one_ref[...] = total.astype(BF16)
    three_ref[...] = (wide(mine, 128, 64) + spread(wide(four, 32, 16), 2)).astype(BF16)


def down_z_body(near, four, back_5, back_7, back_1, back_3, key_ref, value_ref):
    columns = key_ref.shape[1]
    total = near[...] + spread(wide(four, 0, 16), 4) + spread(back_1[...], 1) + spread(back_3[...], 2)
    total = total + spread(wide(back_5, 0, 32) + wide(back_7, 0, 32), 3)
    key_ref[...] = total[:, :columns].astype(BF16)
    value_ref[...] = total[:, columns:].astype(BF16)


def weight_body(*refs):
    lefts, own_grads, other_grads, out_refs, total_ref = refs[:4], refs[4:8], refs[8:12], refs[12:16], refs[16]
    columns = own_grads[0].shape[1]
    me, head = lax.axis_index(Y), lax.axis_index("head")
    for side, rights in ((head, own_grads), (1 - head, other_grads)):
        total = None
        for left, right in zip(lefts, rights):
            part = lax.dot_general(left[...], right[...], TN, preferred_element_type=F32)
            total = part if total is None else total + part
        total_ref[:, cut_at(side, columns)] = total * (1.0 / 32768)
    for mask, ref in enumerate(out_refs):
        ref[...] = total_ref[pl.ds(pl.multiple_of((me ^ mask) * 32, 32), 32)].astype(BF16)


def sum_body(*refs):
    total = wide(refs[0])
    for ref in refs[1:-1]:
        total = total + wide(ref)
    refs[-1][...] = total.astype(BF16)


def join_body(*refs):
    me = lax.axis_index(Y)
    out_ref = refs[4]
    for mask, ref in enumerate(refs[:4]):
        out_ref[pl.ds(pl.multiple_of((me ^ mask) * 32, 32), 32)] = ref[...]


def widen_body(*refs):
    me = lax.axis_index(X)
    out_ref = refs[4]
    for mask, ref in enumerate(refs[:4]):
        out_ref[cut_at(me ^ mask, POOL)] = wide(ref)


def columns_body(weight, out_ref):
    columns = out_ref.shape[1]
    out_ref[...] = weight[:, cut_at(1 - lax.axis_index("head"), columns)]


def grad_in_body(own, other, weight, out_ref):
    columns = own.shape[1]
    head = lax.axis_index("head")
    nt = (((1,), (1,)), ((), ()))
    total = lax.dot_general(own[...], weight[:, cut_at(head, columns)], nt, preferred_element_type=F32)
    total = total + lax.dot_general(
        other[...], weight[:, cut_at(1 - head, columns)], nt, preferred_element_type=F32
    )
    out_ref[...] = total.astype(BF16)


def mixed_body(own, other, weight, other_rows, out_ref):
    columns = own.shape[1]
    own_rows = weight[:, cut_at(lax.axis_index("head"), columns)]
    total = jnp.dot(own[...], own_rows, preferred_element_type=F32)
    total = total + jnp.dot(other[...], other_rows[...], preferred_element_type=F32)
    out_ref[...] = total.astype(BF16)


def per_device(query, key, value, grad_out, out_weight):
    tokens, columns = query.shape
    width = 2 * columns

    def rows(*counts):
        return [((count, width), BF16) for count in counts]

    one, two, three = call(pool_body, rows(128, 64, 32), key, value)
    z_1 = from_partner(one, Z, 1)
    z_3 = from_partner(two, Z, 3)
    grads = [grad_out] + to_others([grad_out] * 3, X, (1, 2, 3))
    two, pair = call(pair_body, rows(64, 64), three, z_1)
    beside_3, z_5, z_7 = to_others((two, pair, pair), Z, (3, 5, 7))
    (other_rows,) = call(columns_body, [((columns, columns), BF16)], out_weight)
    other_rows = from_partner(other_rows, "head", 1)
    four, five = call(
        climb_z_body, rows(128, 64), pair, z_3, beside_3, z_5, z_7, after=grads[1:]
    )
    y_1, y_2, y_3 = to_others((four, five, five), Y, (1, 2, 3))
    six, seven = call(climb_y_body, rows(128, 64), five, y_1, y_2, y_3)
    x_1, x_2, x_3 = to_others((six, seven, seven), X, (1, 2, 3))
    grads[1:] = call(lambda: None, [], through=grads[1:], after=(x_1, x_2, x_3))
    other_grads = [from_partner(grad, "head", 1) for grad in grads]
    (grad_in,) = call(grad_in_body, [((tokens, columns), BF16)], grads[0], other_grads[0], out_weight)
    listed_rows = tokens + 7 * POOL
    attended, probs, listed, *quarters = call(
        forward_body,
        [((tokens, columns), BF16), ((columns // PAIR, 2 * tokens, listed_rows), F32), ((listed_rows, width), BF16)]
        + [((tokens, POOL), BF16)] * 4,
        query, key, value, x_1, x_2, x_3, y_1, y_2, y_3, z_1, z_3, beside_3, z_5, z_7,
        vmem=12,
        after=(other_rows,),
        flops=6 * 10**9,
    )
    quarters = [quarters[0]] + to_others(quarters[1:], X, (1, 2, 3))
    grad_query, near, far_x_1, far_x_2, far_x_3, far_y, far_z = call(
        backward_body,
        [((tokens, columns), BF16), ((tokens, width), F32)] + rows(128, 64, 64, 256, 384),
        query, grad_in, listed, probs,
        vmem=16,
        after=other_grads[1:],
        flops=8 * 10**9,
    )
    *terms, far_x_1, far_x_2, far_x_3 = call(
        weight_body, rows(32, 32, 32, 32), *quarters, *grads, *other_grads,
        scratch=[pltpu.VMEM((POOL, width), F32)],
        through=(far_x_1, far_x_2, far_x_3),
    )
    back_x = to_others((far_x_1, far_x_2, far_x_3), X, (1, 2, 3))
    terms = [terms[0]] + to_others(terms[1:], Y, (1, 2, 3))
    carry, *to_y = call(down_x_body, rows(128, 128, 64, 64), far_y, *back_x)
    back_y = to_others(to_y, Y, (1, 2, 3))
    other_attended = from_partner(attended, "head", 1)
    (term,) = call(sum_body, rows(32), *terms)
    four, beside, to_5, to_7 = call(down_y_body, rows(128, 64, 64, 64), far_z, carry, *back_y)
    beside, back_5, back_7 = to_others((beside, to_5, to_7), Z, (3, 5, 7))
    (term,) = call(sum_body, rows(32), term, *to_others([term] * 3, Z, (3, 5, 6)))
    (term,) = call(sum_body, rows(32), term, from_partner(term, Z, 1))
    (term,) = call(join_body, rows(128), term, *to_others([term] * 3, Y, (1, 2, 3)))
    to_1, to_3 = call(down_pair_body, rows(128, 64), far_z, four, beside, back_5, back_7)
    back_1, back_3 = to_others((to_1, to_3), Z, (1, 3))
    others = to_others([term] * 3, X, (1, 2, 3))
    (mixed,) = call(
        mixed_body, [((tokens, columns), BF16)], attended, other_attended, out_weight, other_rows, after=(four,)
    )
    grad_key, grad_value = call(
        down_z_body, [((tokens, columns), BF16)] * 2, near, four, back_5, back_7, back_1, back_3
    )
    (grad_weight,) = call(widen_body, [((columns, width), F32)], term, *others, vmem=6)
    return mixed, grad_query, grad_key, grad_value, grad_weight


def solution(mesh):
    finer = Mesh(mesh.devices.reshape(4, 4, 8, mesh.shape["head"]), (*SEQ, "head"))
    in_specs = (P(SEQ, "head"), P(SEQ, "head"), P(SEQ, "head"), P(SEQ, "head"), P("head", None))
    return jax.shard_map(
        per_device, mesh=finer, in_specs=in_specs, out_specs=in_specs, check_vma=False
    )
```

```python
import jax
import jax.numpy as jnp
from jax import lax
from jax.experimental import pallas as pl
from jax.experimental.pallas import tpu as pltpu
from jax.sharding import Mesh
from jax.sharding import PartitionSpec as P

HEAD_DIM = 64
POOL = 128
X, Y, Z = "seq_0", "seq_1", "seq_2"
SEQ = (X, Y, Z)
MIB = 1 << 20
F32 = jnp.float32
BF16 = jnp.bfloat16


def from_partner(value, axis, mask):
    pairs = [(source, source ^ mask) for source in range(lax.axis_size(axis))]
    return lax.ppermute(value, axis, pairs)


def to_others(values, axis, masks):
    return [from_partner(value, axis, mask) for value, mask in zip(values, masks)]


def call(body, outs, *args, scratch=(), vmem=4, after=(), through=(), flops=0):
    count, passed = len(args), len(after) + len(through)

    def ordered(*refs):
        made = refs[count + passed :]
        body(*refs[:count], *made[: len(outs)], *made[len(outs) + len(through) :])

    whole, anywhere = pl.BlockSpec(memory_space=pltpu.VMEM), pl.BlockSpec(memory_space=pl.ANY)
    return pl.pallas_call(
        ordered,
        out_shape=tuple(jax.ShapeDtypeStruct(shape, kind) for shape, kind in outs)
        + tuple(jax.ShapeDtypeStruct(value.shape, value.dtype) for value in through),
        in_specs=[whole] * count + [anywhere] * passed,
        out_specs=(whole,) * len(outs) + (anywhere,) * len(through),
        scratch_shapes=list(scratch),
        input_output_aliases={count + len(after) + at: len(outs) + at for at in range(len(through))},
        compiler_params=pltpu.CompilerParams(vmem_limit_bytes=vmem * MIB),
        cost_estimate=pl.CostEstimate(flops=flops, bytes_accessed=0, transcendentals=0) if flops else None,
    )(*args, *after, *through)


def iotas(rows, columns):
    return (
        lax.broadcasted_iota(jnp.int32, (rows, columns), 0),
        lax.broadcasted_iota(jnp.int32, (rows, columns), 1),
    )


def halved(values):
    rows = values.shape[0] // 2
    row, column = iotas(rows, 2 * rows)
    means = jnp.where((column >> 1) == row, 0.5, 0.0).astype(BF16)
    return jnp.dot(means, values, preferred_element_type=F32).astype(BF16)


def spread(values, height):
    values = values.astype(BF16)
    rows = values.shape[0] << height
    row, column = iotas(rows, values.shape[0])
    shares = jnp.where((row >> height) == column, 2.0**-height, 0.0).astype(BF16)
    return jnp.dot(shares, values, preferred_element_type=F32)


def wide(ref, start=0, rows=None):
    rows = ref.shape[0] - start if rows is None else rows
    return ref[start : start + rows].astype(F32)


def cut_at(side, columns):
    return pl.ds(pl.multiple_of(side * columns, columns), columns)


def pool_body(key_ref, value_ref, one_ref, two_ref, three_ref):
    columns = key_ref.shape[1]
    for at, ref in ((0, key_ref), (columns, value_ref)):
        one = halved(ref[...])
        two = halved(one)
        one_ref[:, at : at + columns] = one
        two_ref[:, at : at + columns] = two
        three_ref[:, at : at + columns] = halved(two)


def pair_body(three, from_1, two_ref, pair_ref):
    two = halved(from_1[...])
    two_ref[...] = two
    pair_ref[:32] = three[...]
    pair_ref[32:] = halved(two)


def climb_z_body(pair, from_3, beside_3, from_5, from_7, four_ref, five_ref):
    rows = [pair[...], halved(from_3[...]), halved(beside_3[...]), from_5[...], from_7[...]]
    four = halved(jnp.concatenate(rows, axis=0))
    four_ref[...] = four
    five_ref[...] = halved(four)


def climb_y_body(five, from_1, from_2, from_3, six_ref, seven_ref):
    rows = [five[...], halved(from_1[...]), from_2[...], from_3[...]]
    six = halved(jnp.concatenate(rows, axis=0))
    six_ref[...] = six
    seven_ref[...] = halved(six)


PAIR = 2 * HEAD_DIM
NT = (((1,), (1,)), ((), ()))
TN = (((0,), (0,)), ((), ()))


def first_head(rows):
    return lax.broadcasted_iota(jnp.int32, (rows, PAIR), 1) < HEAD_DIM


def by_head(block):
    first, zero = first_head(block.shape[0]), jnp.zeros_like(block)
    return jnp.concatenate([jnp.where(first, block, zero), jnp.where(first, zero, block)], axis=0)


def side_by_side(block):
    rows = block.shape[0] // 2
    return jnp.where(first_head(rows), block[:rows], block[rows:])


def scaled(block):
    return block * jnp.asarray(HEAD_DIM**-0.5, BF16)


def forward_body(*refs):
    query, key, value = refs[:3]
    pieces = refs[3:14]
    attended_ref, probs_ref, listed = refs[14:17]
    quarter_refs = refs[17:21]
    tokens, columns = query.shape
    listed[:tokens, :columns] = key[...]
    listed[:tokens, columns:] = value[...]
    at = tokens
    for piece in pieces:
        rows = piece.shape[0]
        listed[at : at + rows] = piece[...]
        at += rows
    for pair in range(columns // PAIR):
        cut = slice(pair * PAIR, (pair + 1) * PAIR)
        cut_v = slice(columns + pair * PAIR, columns + (pair + 1) * PAIR)
        queries = by_head(scaled(query[:, cut]))
        scores = lax.dot_general(queries, listed[:, cut], NT, preferred_element_type=F32)
        powers = jnp.exp(scores - jnp.max(scores, axis=1, keepdims=True))
        probs = powers * (1.0 / jnp.sum(powers, axis=1, keepdims=True))
        probs_ref[pair] = probs
        attended_ref[:, cut] = side_by_side(
            jnp.dot(probs.astype(BF16), listed[:, cut_v], preferred_element_type=F32)
        ).astype(BF16)
    me = lax.axis_index(Y)
    for mask, ref in enumerate(quarter_refs):
        ref[...] = attended_ref[:, cut_at(me ^ mask, POOL)]


def backward_body(*refs):
    query, grad, listed, probs_ref = refs[:4]
    grad_query_ref, near_ref = refs[4:6]
    far_refs = refs[6:]
    tokens, columns = query.shape
    for pair in range(columns // PAIR):
        cut = slice(pair * PAIR, (pair + 1) * PAIR)
        cut_v = slice(columns + pair * PAIR, columns + (pair + 1) * PAIR)
        keys, values = listed[:, cut], listed[:, cut_v]
        queries = by_head(scaled(query[:, cut]))
        grads = by_head(grad[:, cut])
        probs = probs_ref[pair]
        weights = probs.astype(BF16)
        grad_probs = lax.dot_general(grads, values, NT, preferred_element_type=F32)
        centred = jnp.sum(probs * grad_probs, axis=1, keepdims=True)
        grad_scores = (probs * (grad_probs - centred)).astype(BF16)
        grad_query_ref[:, cut] = (
            side_by_side(jnp.dot(grad_scores, keys, preferred_element_type=F32)) * HEAD_DIM**-0.5
        ).astype(BF16)
        for where, left, right in ((cut, grad_scores, queries), (cut_v, weights, grads)):
            total = lax.dot_general(left, right, TN, preferred_element_type=F32)
            near_ref[:, where] = total[:tokens]
            at = tokens
            for ref in far_refs:
                rows = ref.shape[0]
                ref[:, where] = total[at : at + rows].astype(BF16)
                at += rows


def down_x_body(mine, own_term, back_1, back_2, back_3, carry_ref, one_ref, two_ref, three_ref, term_ref):
    six = wide(back_1, 0, 128) + spread(wide(back_2, 0, 64) + wide(back_3, 0, 64), 1)
    carry_ref[...] = spread(six[:32], 2).astype(BF16)
    one_ref[...] = (wide(mine, 0, 128) + spread(six[32:64], 2)).astype(BF16)
    two_ref[...] = (wide(mine, 128, 64) + spread(six[64:96], 1)).astype(BF16)
    three_ref[...] = (wide(mine, 192, 64) + spread(six[96:], 1)).astype(BF16)
    term = wide(own_term) + wide(back_1, 128, 32) + wide(back_2, 64, 32) + wide(back_3, 64, 32)
    term_ref[...] = term.astype(BF16)


def down_y_body(mine, carry, back_1, back_2, back_3, four_ref, beside_ref, five_ref, seven_ref):
    four = wide(carry) + wide(back_1) + spread(wide(back_2) + wide(back_3), 1)
    four_ref[...] = four.astype(BF16)
    beside_ref[...] = (wide(mine, 192, 64) + spread(four[48:64], 2)).astype(BF16)
    five_ref[...] = (wide(mine, 256, 64) + spread(four[64:96], 1)).astype(BF16)
    seven_ref[...] = (wide(mine, 320, 64) + spread(four[96:], 1)).astype(BF16)


def down_pair_body(mine, four, beside, back_5, back_7, one_ref, three_ref):
    total = wide(mine, 0, 128) + spread(wide(four, 16, 16), 3) + spread(beside[...], 1)
    total = total + spread(wide(back_5, 32, 32) + wide(back_7, 32, 32), 2)
    one_ref[...] = total.astype(BF16)
    three_ref[...] = (wide(mine, 128, 64) + spread(wide(four, 32, 16), 2)).astype(BF16)


def down_z_body(near, four, back_5, back_7, back_1, back_3, key_ref, value_ref):
    columns = key_ref.shape[1]
    total = near[...] + spread(wide(four, 0, 16), 4) + spread(back_1[...], 1) + spread(back_3[...], 2)
    total = total + spread(wide(back_5, 0, 32) + wide(back_7, 0, 32), 3)
    key_ref[...] = total[:, :columns].astype(BF16)
    value_ref[...] = total[:, columns:].astype(BF16)


def weight_body(*refs):
    lefts, own_grads, other_grads, far_refs = refs[:4], refs[4:8], refs[8:12], refs[12:15]
    out_refs, total_ref = refs[15:19], refs[19]
    columns = own_grads[0].shape[1]
    me, head = lax.axis_index(X), lax.axis_index("head")
    for side, rights in ((head, own_grads), (1 - head, other_grads)):
        total = None
        for left, right in zip(lefts, rights):
            part = lax.dot_general(left[...], right[...], TN, preferred_element_type=F32)
            total = part if total is None else total + part
        total_ref[:, cut_at(side, columns)] = total * (1.0 / 32768)
    for mask, ref in enumerate(out_refs):
        rows = ref.shape[0] - 32
        if mask:
            ref[:rows] = far_refs[mask - 1][...]
        ref[rows:] = total_ref[pl.ds(pl.multiple_of((me ^ mask) * 32, 32), 32)].astype(BF16)


def sum_body(*refs):
    total = wide(refs[0])
    for ref in refs[1:-1]:
        total = total + wide(ref)
    refs[-1][...] = total.astype(BF16)


def join_body(*refs):
    me = lax.axis_index(X)
    out_ref = refs[4]
    for mask, ref in enumerate(refs[:4]):
        out_ref[pl.ds(pl.multiple_of((me ^ mask) * 32, 32), 32)] = ref[...]


def widen_body(*refs):
    me = lax.axis_index(Y)
    out_ref = refs[4]
    for mask, ref in enumerate(refs[:4]):
        out_ref[cut_at(me ^ mask, POOL)] = wide(ref)


def columns_body(weight, out_ref):
    columns = out_ref.shape[1]
    out_ref[...] = weight[:, cut_at(1 - lax.axis_index("head"), columns)]


def grad_in_body(own, other, weight, out_ref):
    columns = own.shape[1]
    head = lax.axis_index("head")
    nt = (((1,), (1,)), ((), ()))
    total = lax.dot_general(own[...], weight[:, cut_at(head, columns)], nt, preferred_element_type=F32)
    total = total + lax.dot_general(
        other[...], weight[:, cut_at(1 - head, columns)], nt, preferred_element_type=F32
    )
    out_ref[...] = total.astype(BF16)


def mixed_body(own, other, weight, other_rows, out_ref):
    columns = own.shape[1]
    own_rows = weight[:, cut_at(lax.axis_index("head"), columns)]
    total = jnp.dot(own[...], own_rows, preferred_element_type=F32)
    total = total + jnp.dot(other[...], other_rows[...], preferred_element_type=F32)
    out_ref[...] = total.astype(BF16)


def per_device(query, key, value, grad_out, out_weight):
    tokens, columns = query.shape
    width = 2 * columns

    def rows(*counts):
        return [((count, width), BF16) for count in counts]

    one, two, three = call(pool_body, rows(128, 64, 32), key, value)
    z_1 = from_partner(one, Z, 1)
    z_3 = from_partner(two, Z, 3)
    grads = [grad_out] + to_others([grad_out] * 3, Y, (1, 2, 3))
    two, pair = call(pair_body, rows(64, 64), three, z_1)
    beside_3, z_5, z_7 = to_others((two, pair, pair), Z, (3, 5, 7))
    (other_rows,) = call(columns_body, [((columns, columns), BF16)], out_weight)
    other_rows = from_partner(other_rows, "head", 1)
    four, five = call(
        climb_z_body, rows(128, 64), pair, z_3, beside_3, z_5, z_7, after=grads[1:]
    )
    y_1, y_2, y_3 = to_others((four, five, five), Y, (1, 2, 3))
    six, seven = call(climb_y_body, rows(128, 64), five, y_1, y_2, y_3)
    x_1, x_2, x_3 = to_others((six, seven, seven), X, (1, 2, 3))
    grads[1:] = call(lambda: None, [], through=grads[1:], after=(x_1, x_2, x_3))
    other_grads = [from_partner(grad, "head", 1) for grad in grads]
    (grad_in,) = call(grad_in_body, [((tokens, columns), BF16)], grads[0], other_grads[0], out_weight)
    listed_rows = tokens + 7 * POOL
    attended, probs, listed, *quarters = call(
        forward_body,
        [((tokens, columns), BF16), ((columns // PAIR, 2 * tokens, listed_rows), F32), ((listed_rows, width), BF16)]
        + [((tokens, POOL), BF16)] * 4,
        query, key, value, x_1, x_2, x_3, y_1, y_2, y_3, z_1, z_3, beside_3, z_5, z_7,
        vmem=12,
        after=(other_rows,),
        flops=6 * 10**9,
    )
    quarters = [quarters[0]] + to_others(quarters[1:], Y, (1, 2, 3))
    grad_query, near, far_x_1, far_x_2, far_x_3, far_y, far_z = call(
        backward_body,
        [((tokens, columns), BF16), ((tokens, width), F32)] + rows(128, 64, 64, 256, 384),
        query, grad_in, listed, probs,
        vmem=16,
        after=other_grads[1:],
        flops=8 * 10**9,
    )
    own_term, *to_x = call(
        weight_body, rows(32, 160, 96, 96), *quarters, *grads, *other_grads, far_x_1, far_x_2, far_x_3,
        scratch=[pltpu.VMEM((POOL, width), F32)],
    )
    back_x = to_others(to_x, X, (1, 2, 3))
    carry, *to_y, term = call(down_x_body, rows(128, 128, 64, 64, 32), far_y, own_term, *back_x)
    back_y = to_others(to_y, Y, (1, 2, 3))
    other_attended = from_partner(attended, "head", 1)
    four, beside, to_5, to_7 = call(down_y_body, rows(128, 64, 64, 64), far_z, carry, *back_y)
    beside, back_5, back_7 = to_others((beside, to_5, to_7), Z, (3, 5, 7))
    (term,) = call(sum_body, rows(32), term, *to_others([term] * 3, Z, (3, 5, 6)))
    (term,) = call(sum_body, rows(32), term, from_partner(term, Z, 1))
    (term,) = call(join_body, rows(128), term, *to_others([term] * 3, X, (1, 2, 3)))
    to_1, to_3 = call(down_pair_body, rows(128, 64), far_z, four, beside, back_5, back_7)
    back_1, back_3 = to_others((to_1, to_3), Z, (1, 3))
    others = to_others([term] * 3, Y, (1, 2, 3))
    (mixed,) = call(
        mixed_body, [((tokens, columns), BF16)], attended, other_attended, out_weight, other_rows, after=(four,)
    )
    grad_key, grad_value = call(
        down_z_body, [((tokens, columns), BF16)] * 2, near, four, back_5, back_7, back_1, back_3
    )
    (grad_weight,) = call(widen_body, [((columns, width), F32)], term, *others, vmem=6)
    return mixed, grad_query, grad_key, grad_value, grad_weight


def solution(mesh):
    finer = Mesh(mesh.devices.reshape(4, 4, 8, mesh.shape["head"]), (*SEQ, "head"))
    in_specs = (P(SEQ, "head"), P(SEQ, "head"), P(SEQ, "head"), P(SEQ, "head"), P("head", None))
    return jax.shard_map(
        per_device, mesh=finer, in_specs=in_specs, out_specs=in_specs, check_vma=False
    )
```

```python
import jax
import jax.numpy as jnp
from jax import lax
from jax.experimental import pallas as pl
from jax.experimental.pallas import tpu as pltpu
from jax.sharding import Mesh
from jax.sharding import PartitionSpec as P

HEAD_DIM = 64
POOL = 128
X, Y, Z = "seq_0", "seq_1", "seq_2"
SEQ = (X, Y, Z)
MIB = 1 << 20
F32 = jnp.float32
BF16 = jnp.bfloat16


def from_partner(value, axis, mask):
    pairs = [(source, source ^ mask) for source in range(lax.axis_size(axis))]
    return lax.ppermute(value, axis, pairs)


def to_others(values, axis, masks):
    return [from_partner(value, axis, mask) for value, mask in zip(values, masks)]


def call(body, outs, *args, scratch=(), vmem=4, after=(), through=(), flops=0):
    count, passed = len(args), len(after) + len(through)

    def ordered(*refs):
        made = refs[count + passed :]
        body(*refs[:count], *made[: len(outs)], *made[len(outs) + len(through) :])

    whole, anywhere = pl.BlockSpec(memory_space=pltpu.VMEM), pl.BlockSpec(memory_space=pl.ANY)
    return pl.pallas_call(
        ordered,
        out_shape=tuple(jax.ShapeDtypeStruct(shape, kind) for shape, kind in outs)
        + tuple(jax.ShapeDtypeStruct(value.shape, value.dtype) for value in through),
        in_specs=[whole] * count + [anywhere] * passed,
        out_specs=(whole,) * len(outs) + (anywhere,) * len(through),
        scratch_shapes=list(scratch),
        input_output_aliases={count + len(after) + at: len(outs) + at for at in range(len(through))},
        compiler_params=pltpu.CompilerParams(vmem_limit_bytes=vmem * MIB),
        cost_estimate=pl.CostEstimate(flops=flops, bytes_accessed=0, transcendentals=0) if flops else None,
    )(*args, *after, *through)


def iotas(rows, columns):
    return (
        lax.broadcasted_iota(jnp.int32, (rows, columns), 0),
        lax.broadcasted_iota(jnp.int32, (rows, columns), 1),
    )


def halved(values):
    rows = values.shape[0] // 2
    row, column = iotas(rows, 2 * rows)
    means = jnp.where((column >> 1) == row, 0.5, 0.0).astype(BF16)
    return jnp.dot(means, values, preferred_element_type=F32).astype(BF16)


def spread(values, height):
    values = values.astype(BF16)
    rows = values.shape[0] << height
    row, column = iotas(rows, values.shape[0])
    shares = jnp.where((row >> height) == column, 2.0**-height, 0.0).astype(BF16)
    return jnp.dot(shares, values, preferred_element_type=F32)


def wide(ref, start=0, rows=None):
    rows = ref.shape[0] - start if rows is None else rows
    return ref[start : start + rows].astype(F32)


def cut_at(side, columns):
    return pl.ds(pl.multiple_of(side * columns, columns), columns)


def pool_body(key_ref, value_ref, one_ref, two_ref, three_ref):
    columns = key_ref.shape[1]
    for at, ref in ((0, key_ref), (columns, value_ref)):
        one = halved(ref[...])
        two = halved(one)
        one_ref[:, at : at + columns] = one
        two_ref[:, at : at + columns] = two
        three_ref[:, at : at + columns] = halved(two)


def pair_body(three, from_1, two_ref, pair_ref):
    two = halved(from_1[...])
    two_ref[...] = two
    pair_ref[:32] = three[...]
    pair_ref[32:] = halved(two)


def climb_z_body(pair, from_3, beside_3, from_5, from_7, four_ref, five_ref):
    rows = [pair[...], halved(from_3[...]), halved(beside_3[...]), from_5[...], from_7[...]]
    four = halved(jnp.concatenate(rows, axis=0))
    four_ref[...] = four
    five_ref[...] = halved(four)


def climb_y_body(five, from_1, from_2, from_3, six_ref, seven_ref):
    rows = [five[...], halved(from_1[...]), from_2[...], from_3[...]]
    six = halved(jnp.concatenate(rows, axis=0))
    six_ref[...] = six
    seven_ref[...] = halved(six)


PAIR = 2 * HEAD_DIM
NT = (((1,), (1,)), ((), ()))
TN = (((0,), (0,)), ((), ()))


def first_head(rows):
    return lax.broadcasted_iota(jnp.int32, (rows, PAIR), 1) < HEAD_DIM


def by_head(block):
    first, zero = first_head(block.shape[0]), jnp.zeros_like(block)
    return jnp.concatenate([jnp.where(first, block, zero), jnp.where(first, zero, block)], axis=0)


def side_by_side(block):
    rows = block.shape[0] // 2
    return jnp.where(first_head(rows), block[:rows], block[rows:])


def scaled(block):
    return block * jnp.asarray(HEAD_DIM**-0.5, BF16)


def forward_body(*refs):
    query, key, value = refs[:3]
    pieces = refs[3:14]
    attended_ref, probs_ref, listed = refs[14:17]
    quarter_refs = refs[17:21]
    tokens, columns = query.shape
    listed[:tokens, :columns] = key[...]
    listed[:tokens, columns:] = value[...]
    at = tokens
    for piece in pieces:
        rows = piece.shape[0]
        listed[at : at + rows] = piece[...]
        at += rows
    for pair in range(columns // PAIR):
        cut = slice(pair * PAIR, (pair + 1) * PAIR)
        cut_v = slice(columns + pair * PAIR, columns + (pair + 1) * PAIR)
        queries = by_head(scaled(query[:, cut]))
        scores = lax.dot_general(queries, listed[:, cut], NT, preferred_element_type=F32)
        powers = jnp.exp(scores - jnp.max(scores, axis=1, keepdims=True))
        probs = powers * (1.0 / jnp.sum(powers, axis=1, keepdims=True))
        probs_ref[pair] = probs
        attended_ref[:, cut] = side_by_side(
            jnp.dot(probs.astype(BF16), listed[:, cut_v], preferred_element_type=F32)
        ).astype(BF16)
    me = lax.axis_index(Y)
    for mask, ref in enumerate(quarter_refs):
        ref[...] = attended_ref[:, cut_at(me ^ mask, POOL)]


def backward_body(*refs):
    query, grad, listed, probs_ref = refs[:4]
    grad_query_ref, near_ref = refs[4:6]
    far_refs = refs[6:]
    tokens, columns = query.shape
    for pair in range(columns // PAIR):
        cut = slice(pair * PAIR, (pair + 1) * PAIR)
        cut_v = slice(columns + pair * PAIR, columns + (pair + 1) * PAIR)
        keys, values = listed[:, cut], listed[:, cut_v]
        queries = by_head(scaled(query[:, cut]))
        grads = by_head(grad[:, cut])
        probs = probs_ref[pair]
        weights = probs.astype(BF16)
        grad_probs = lax.dot_general(grads, values, NT, preferred_element_type=F32)
        centred = jnp.sum(probs * grad_probs, axis=1, keepdims=True)
        grad_scores = (probs * (grad_probs - centred)).astype(BF16)
        grad_query_ref[:, cut] = (
            side_by_side(jnp.dot(grad_scores, keys, preferred_element_type=F32)) * HEAD_DIM**-0.5
        ).astype(BF16)
        for where, left, right in ((cut, grad_scores, queries), (cut_v, weights, grads)):
            total = lax.dot_general(left, right, TN, preferred_element_type=F32)
            near_ref[:, where] = total[:tokens]
            at = tokens
            for ref in far_refs:
                rows = ref.shape[0]
                ref[:, where] = total[at : at + rows].astype(BF16)
                at += rows


def down_x_body(mine, own_term, back_1, back_2, back_3, carry_ref, one_ref, two_ref, three_ref, term_ref):
    six = wide(back_1, 0, 128) + spread(wide(back_2, 0, 64) + wide(back_3, 0, 64), 1)
    carry_ref[...] = spread(six[:32], 2).astype(BF16)
    one_ref[...] = (wide(mine, 0, 128) + spread(six[32:64], 2)).astype(BF16)
    two_ref[...] = (wide(mine, 128, 64) + spread(six[64:96], 1)).astype(BF16)
    three_ref[...] = (wide(mine, 192, 64) + spread(six[96:], 1)).astype(BF16)
    term = wide(own_term) + wide(back_1, 128, 32) + wide(back_2, 64, 32) + wide(back_3, 64, 32)
    term_ref[...] = term.astype(BF16)


def down_y_body(mine, carry, back_1, back_2, back_3, four_ref, beside_ref, five_ref, seven_ref):
    four = wide(carry) + wide(back_1) + spread(wide(back_2) + wide(back_3), 1)
    four_ref[...] = four.astype(BF16)
    beside_ref[...] = (wide(mine, 192, 64) + spread(four[48:64], 2)).astype(BF16)
    five_ref[...] = (wide(mine, 256, 64) + spread(four[64:96], 1)).astype(BF16)
    seven_ref[...] = (wide(mine, 320, 64) + spread(four[96:], 1)).astype(BF16)


def down_pair_body(mine, four, beside, back_5, back_7, one_ref, three_ref):
    total = wide(mine, 0, 128) + spread(wide(four, 16, 16), 3) + spread(beside[...], 1)
    total = total + spread(wide(back_5, 32, 32) + wide(back_7, 32, 32), 2)
    one_ref[...] = total.astype(BF16)
    three_ref[...] = (wide(mine, 128, 64) + spread(wide(four, 32, 16), 2)).astype(BF16)


def down_z_body(near, four, back_5, back_7, back_1, back_3, key_ref, value_ref):
    columns = key_ref.shape[1]
    total = near[...] + spread(wide(four, 0, 16), 4) + spread(back_1[...], 1) + spread(back_3[...], 2)
    total = total + spread(wide(back_5, 0, 32) + wide(back_7, 0, 32), 3)
    key_ref[...] = total[:, :columns].astype(BF16)
    value_ref[...] = total[:, columns:].astype(BF16)


def weight_body(*refs):
    lefts, own_grads, other_grads, far_refs = refs[:4], refs[4:8], refs[8:12], refs[12:15]
    out_refs, total_ref = refs[15:19], refs[19]
    columns = own_grads[0].shape[1]
    me, head = lax.axis_index(X), lax.axis_index("head")
    for side, rights in ((head, own_grads), (1 - head, other_grads)):
        total = None
        for left, right in zip(lefts, rights):
            part = lax.dot_general(left[...], right[...], TN, preferred_element_type=F32)
            total = part if total is None else total + part
        total_ref[:, cut_at(side, columns)] = total * (1.0 / 32768)
    for mask, ref in enumerate(out_refs):
        rows = ref.shape[0] - 32
        if mask:
            ref[:rows] = far_refs[mask - 1][...]
        ref[rows:] = total_ref[pl.ds(pl.multiple_of((me ^ mask) * 32, 32), 32)].astype(BF16)


def sum_body(*refs):
    total = wide(refs[0])
    for ref in refs[1:-1]:
        total = total + wide(ref)
    refs[-1][...] = total.astype(BF16)


def join_body(*refs):
    me = lax.axis_index(X)
    out_ref = refs[4]
    for mask, ref in enumerate(refs[:4]):
        out_ref[pl.ds(pl.multiple_of((me ^ mask) * 32, 32), 32)] = ref[...]


def widen_body(*refs):
    me = lax.axis_index(Y)
    out_ref = refs[4]
    for mask, ref in enumerate(refs[:4]):
        out_ref[cut_at(me ^ mask, POOL)] = wide(ref)


def columns_body(weight, out_ref):
    columns = out_ref.shape[1]
    out_ref[...] = weight[:, cut_at(1 - lax.axis_index("head"), columns)]


def grad_in_body(own, other, weight, out_ref):
    columns = own.shape[1]
    head = lax.axis_index("head")
    nt = (((1,), (1,)), ((), ()))
    total = lax.dot_general(own[...], weight[:, cut_at(head, columns)], nt, preferred_element_type=F32)
    total = total + lax.dot_general(
        other[...], weight[:, cut_at(1 - head, columns)], nt, preferred_element_type=F32
    )
    out_ref[...] = total.astype(BF16)


def mixed_body(own, other, weight, other_rows, out_ref):
    columns = own.shape[1]
    own_rows = weight[:, cut_at(lax.axis_index("head"), columns)]
    total = jnp.dot(own[...], own_rows, preferred_element_type=F32)
    total = total + jnp.dot(other[...], other_rows[...], preferred_element_type=F32)
    out_ref[...] = total.astype(BF16)


def per_device(query, key, value, grad_out, out_weight):
    tokens, columns = query.shape
    width = 2 * columns

    def rows(*counts):
        return [((count, width), BF16) for count in counts]

    one, two, three = call(pool_body, rows(128, 64, 32), key, value)
    z_1 = from_partner(one, Z, 1)
    z_3 = from_partner(two, Z, 3)
    grads = [grad_out] + to_others([grad_out] * 3, Y, (1, 2, 3))
    two, pair = call(pair_body, rows(64, 64), three, z_1)
    beside_3, z_5, z_7 = to_others((two, pair, pair), Z, (3, 5, 7))
    (other_rows,) = call(columns_body, [((columns, columns), BF16)], out_weight)
    other_rows = from_partner(other_rows, "head", 1)
    four, five = call(
        climb_z_body, rows(128, 64), pair, z_3, beside_3, z_5, z_7, after=grads[1:]
    )
    y_1, y_2, y_3 = to_others((four, five, five), Y, (1, 2, 3))
    six, seven = call(climb_y_body, rows(128, 64), five, y_1, y_2, y_3)
    x_1, x_2, x_3 = to_others((six, seven, seven), X, (1, 2, 3))
    grads[1:] = call(lambda: None, [], through=grads[1:], after=(x_1, x_2, x_3))
    other_grads = [from_partner(grad, "head", 1) for grad in grads]
    (grad_in,) = call(grad_in_body, [((tokens, columns), BF16)], grads[0], other_grads[0], out_weight)
    listed_rows = tokens + 7 * POOL
    attended, probs, listed, *quarters = call(
        forward_body,
        [((tokens, columns), BF16), ((columns // PAIR, 2 * tokens, listed_rows), F32), ((listed_rows, width), BF16)]
        + [((tokens, POOL), BF16)] * 4,
        query, key, value, x_1, x_2, x_3, y_1, y_2, y_3, z_1, z_3, beside_3, z_5, z_7,
        vmem=12,
        after=(other_rows,),
        flops=6 * 10**9,
    )
    quarters = [quarters[0]] + to_others(quarters[1:], Y, (1, 2, 3))
    grad_query, near, far_x_1, far_x_2, far_x_3, far_y, far_z = call(
        backward_body,
        [((tokens, columns), BF16), ((tokens, width), F32)] + rows(128, 64, 64, 256, 384),
        query, grad_in, listed, probs,
        vmem=16,
        after=other_grads[1:],
        flops=8 * 10**9,
    )
    own_term, *to_x = call(
        weight_body, rows(32, 160, 96, 96), *quarters, *grads, *other_grads, far_x_1, far_x_2, far_x_3,
        scratch=[pltpu.VMEM((POOL, width), F32)],
    )
    back_x = to_others(to_x, X, (1, 2, 3))
    carry, *to_y, term, attended = call(
        down_x_body, rows(128, 128, 64, 64, 32), far_y, own_term, *back_x, through=(attended,)
    )
    back_y = to_others(to_y, Y, (1, 2, 3))
    other_attended = from_partner(attended, "head", 1)
    (term,) = call(lambda: None, [], through=(term,), after=(other_attended,))
    four, beside, to_5, to_7 = call(down_y_body, rows(128, 64, 64, 64), far_z, carry, *back_y)
    beside, back_5, back_7 = to_others((beside, to_5, to_7), Z, (3, 5, 7))
    (term,) = call(sum_body, rows(32), term, *to_others([term] * 3, Z, (3, 5, 6)))
    (term,) = call(sum_body, rows(32), term, from_partner(term, Z, 1))
    (term,) = call(join_body, rows(128), term, *to_others([term] * 3, X, (1, 2, 3)))
    to_1, to_3 = call(down_pair_body, rows(128, 64), far_z, four, beside, back_5, back_7)
    back_1, back_3 = to_others((to_1, to_3), Z, (1, 3))
    others = to_others([term] * 3, Y, (1, 2, 3))
    (mixed,) = call(
        mixed_body, [((tokens, columns), BF16)], attended, other_attended, out_weight, other_rows, after=(four,)
    )
    grad_key, grad_value = call(
        down_z_body, [((tokens, columns), BF16)] * 2, near, four, back_5, back_7, back_1, back_3
    )
    (grad_weight,) = call(widen_body, [((columns, width), F32)], term, *others, vmem=6)
    return mixed, grad_query, grad_key, grad_value, grad_weight


def solution(mesh):
    finer = Mesh(mesh.devices.reshape(4, 4, 8, mesh.shape["head"]), (*SEQ, "head"))
    in_specs = (P(SEQ, "head"), P(SEQ, "head"), P(SEQ, "head"), P(SEQ, "head"), P("head", None))
    return jax.shard_map(
        per_device, mesh=finer, in_specs=in_specs, out_specs=in_specs, check_vma=False
    )
```
